128 devices in a mesh: section: 4 (over x_lo, core), mp: 32 (over z, x_hi, y).
Axes of the slice: x: 4 (x_hi: 2, x_lo: 2; x = x_hi * 2 + x_lo), y: 4, z: 4, core: 2. Of those that a mesh axis runs over, the one named last changes fastest.
Arguments:
- tokens: bfloat16 [4, 256, 8192], P('section', 'mp'), may hold values from -6 to 6
- upstream: bfloat16 [4, 256, 8192], P('section', 'mp'), may hold values from -6 to 6
- norm_gain: float32 [4, 8192], P('section'), may hold values from 0.1 to 1.9
- w_query: bfloat16 [4, 8192, 8192], P('section', None, 'mp'), may hold values from -0.0625 to 0.0625
- w_output: bfloat16 [4, 8192, 8192], P('section', 'mp'), may hold values from -0.0625 to 0.0625
- w_keyvalue: bfloat16 [4, 7680, 2048], P('section', 'mp'), may hold values from -0.0625 to 0.0625
- image_feats: bfloat16 [512, 7680], P(('section', 'mp')), may hold values from -20 to 20
- visible: int32 [2], replicated, may hold values from 1 to 4, as said below
Outputs:
- grad_tokens: bfloat16 [4, 256, 8192], P('section', 'mp')
- grad_gain: float32 [4, 8192], P('section')
- grad_query: bfloat16 [4, 8192, 8192], P('section', None, 'mp')
- grad_output: bfloat16 [4, 8192, 8192], P('section', 'mp')
- grad_keyvalue: bfloat16 [4, 7680, 2048], P('section', 'mp')
- grad_image: float32 [512, 7680], P(('section', 'mp'))
The draws below stay inside these ranges and needn't reach their ends.
Inputs may be any that keep to these rules, and one draw needn't show every extreme that they name: `visible`: never falls from block to block; the last block sees all 4 images.
All inputs are finite; a program needn't handle non-finite values.
Results may differ from the reference program's by a relative error of at most 0.014.
The reference program's roundings to bfloat16 on the way count: a program that leaves them out, or rounds other values in their place, can miss the bound.
Values may be sent and summed in bfloat16 or wider, within the bound.
A program may use at most 128 MiB of HBM per device.

```python
import math
import jax
import jax.numpy as jnp
from jax import lax

D = 8192
VD = 7680
HD = 128
GROUP = 8
HEADS_DEV = 2
IMAGES = 4
BLOCK = 128
TOK = 256
VROWS = 128
H = 64
KVH = 8
R = 512
SECTIONS = 4


def draw_visible(key, part):
    key = jax.random.fold_in(key, 7)
    raw = jax.random.randint(key, (TOK // BLOCK,), 1, IMAGES + 1)
    ordered = jnp.sort(raw)
    return ordered.at[-1].set(IMAGES).astype(jnp.int32)


def draw_image_feats(key, part):
    key = jax.random.fold_in(key, 11)
    first, second = jax.random.split(key)
    spread = jnp.exp(jax.random.uniform(second, (R, 1), jnp.float32, 0.0, math.log(4.0)))
    values = jnp.clip(jax.random.normal(first, (R, VD), jnp.float32) * spread, -20.0, 20.0)
    return values.astype(jnp.bfloat16)


def levels(rng, dims, shards, low, largest):
    gain = 1.0
    for axis_at, blocks in shards:
        steps = jax.random.uniform(jax.random.fold_in(jax.random.fold_in(rng, 6), axis_at), (blocks,), jnp.float32, low / len(shards), largest / len(shards))
        gain = gain * jnp.repeat(jnp.exp(steps), dims[axis_at] // blocks).reshape((-1,) + (1,) * (len(dims) - 1 - axis_at))
    return gain


def gaussian(rng, shape, scale, reach, cuts=(), kind=jnp.bfloat16):
    values = jax.random.normal(rng, shape, jnp.float32) * scale
    if len(cuts) > 0:
        values = levels(rng, shape, cuts, -0.22, 0.18) * values
    return jnp.clip(values, min=-reach, max=reach).astype(kind)


def setup_inputs(seed: int = 0) -> dict:
    arg_keys = jax.random.split(jax.random.key(seed), 9)
    return {
        "tokens": gaussian(arg_keys[0], (SECTIONS, TOK, D), 1.0, 6.0, ((0, 4), (1, 32))),
        "upstream": gaussian(arg_keys[1], (SECTIONS, TOK, D), 1.0, 6.0, ((0, 4), (1, 32))),
        "norm_gain": jnp.clip(1.0 + 0.18 * jax.random.normal(arg_keys[2], (SECTIONS, D), jnp.float32), 0.1, 1.9),
        "w_query": gaussian(arg_keys[3], (SECTIONS, D, H * HD), D ** -0.5, 0.0625, ((0, 4), (2, 32))),
        "w_output": gaussian(arg_keys[4], (SECTIONS, H * HD, D), (H * HD) ** -0.5, 0.0625, ((0, 4), (1, 32))),
        "w_keyvalue": gaussian(arg_keys[5], (SECTIONS, VD, 2 * KVH * HD), VD ** -0.5, 0.0625, ((0, 4), (1, 32))),
        "image_feats": draw_image_feats(jax.random.fold_in(arg_keys[8], 71), 0),
        "visible": draw_visible(jax.random.fold_in(arg_keys[8], 71), 0),
    }


def rounded(value):
    return lax.optimization_barrier(value.astype(jnp.bfloat16)).astype(jnp.float32)

def pair_sums(grads):
    runs = GROUP // HEADS_DEV
    shaped = grads.reshape(R, KVH, runs, HEADS_DEV, HD)
    partial_sums = rounded(lax.optimization_barrier(jnp.sum(shaped, axis=3)))
    return lax.optimization_barrier(jnp.sum(partial_sums, axis=2)).astype(jnp.bfloat16).reshape(R, KVH * HD)

def layer_grads(inputs, cotangent, gain_row, w_q, w_o, w_kv, feats, allowed):
    xfloat = inputs.astype(jnp.float32)
    rinv = lax.rsqrt(lax.optimization_barrier(jnp.mean(xfloat * xfloat, axis=-1, keepdims=True)) + 1e-05)
    normed = (xfloat * rinv * gain_row[None, :]).astype(jnp.bfloat16)
    query = jnp.dot(normed, w_q, preferred_element_type=jnp.float32).astype(jnp.bfloat16)
    keyvalue = jnp.dot(feats, w_kv, preferred_element_type=jnp.float32).astype(jnp.bfloat16)
    width = KVH * HD
    keys = keyvalue[:, :width].astype(jnp.float32).reshape(R, KVH, HD)
    values = keyvalue[:, width:].astype(jnp.float32).reshape(R, KVH, HD)
    queries = query.astype(jnp.float32).reshape(TOK, KVH, GROUP, HD)
    scale = HD ** (-0.5)
    scores = jnp.einsum('tkgd,rkd->kgtr', queries, keys) * scale
    scores = jnp.where(allowed[None, None], scores, -1e+30)
    top = lax.optimization_barrier(jnp.max(scores, axis=-1, keepdims=True))
    expo = jnp.exp(scores - top)
    probs = expo / lax.optimization_barrier(jnp.sum(expo, axis=-1, keepdims=True))
    weights = rounded(probs)
    attn = jnp.einsum('kgtr,rkd->tkgd', weights, values).astype(jnp.bfloat16).reshape(TOK, KVH * GROUP * HD)
    grad_out = jnp.dot(attn.T, cotangent, preferred_element_type=jnp.float32).astype(jnp.bfloat16)
    d_attn = rounded(jnp.dot(cotangent, w_o.T, preferred_element_type=jnp.float32)).reshape(TOK, KVH, GROUP, HD)
    d_prob = jnp.einsum('tkgd,rkd->kgtr', d_attn, values)
    d_value = jnp.einsum('kgtr,tkgd->rkgd', weights, d_attn)
    delta = lax.optimization_barrier(jnp.sum(probs * d_prob, axis=-1, keepdims=True))
    d_score = rounded(probs * (d_prob - delta) * scale)
    d_query = jnp.einsum('kgtr,rkd->tkgd', d_score, keys).astype(jnp.bfloat16).reshape(TOK, KVH * GROUP * HD)
    d_key = jnp.einsum('kgtr,tkgd->rkgd', d_score, queries)
    d_keyvalue = jnp.concatenate([pair_sums(d_key), pair_sums(d_value)], axis=1)
    grad_q = jnp.dot(normed.T, d_query, preferred_element_type=jnp.float32).astype(jnp.bfloat16)
    grad_kv = jnp.dot(feats.T, d_keyvalue, preferred_element_type=jnp.float32).astype(jnp.bfloat16)
    d_feats = jnp.dot(d_keyvalue, w_kv.T, preferred_element_type=jnp.float32)
    d_normed = jnp.dot(d_query, w_q.T, preferred_element_type=jnp.float32)
    scaled = d_normed * gain_row[None, :]
    grad_g = lax.optimization_barrier(jnp.sum(d_normed * xfloat * rinv, axis=0))
    grad_x = rinv * scaled - xfloat * rinv * rinv * rinv * lax.optimization_barrier(jnp.mean(xfloat * scaled, axis=-1, keepdims=True))
    return (grad_x.astype(jnp.bfloat16), grad_g, grad_q, grad_out, grad_kv, d_feats)

def reference(tokens, upstream, norm_gain, w_query, w_output, w_keyvalue, image_feats, visible):
    image_of = jnp.arange(R, dtype=jnp.int32) // VROWS
    seen = jnp.repeat(visible, BLOCK)
    allowed = image_of[None, :] < seen[:, None]
    grad_x_all, grad_g_all, grad_q_all, grad_o_all, grad_kv_all = ([], [], [], [], [])
    feat_total = jnp.zeros((R, VD), jnp.float32)
    for layer in range(SECTIONS):
        grad_x, grad_g, grad_q, grad_out, grad_kv, d_feats = layer_grads(tokens[layer], upstream[layer], norm_gain[layer], w_query[layer], w_output[layer], w_keyvalue[layer], image_feats, allowed)
        grad_x_all.append(grad_x)
        grad_g_all.append(grad_g)
        grad_q_all.append(grad_q)
        grad_o_all.append(grad_out)
        grad_kv_all.append(grad_kv)
        feat_total = feat_total + d_feats
    return (jnp.stack(grad_x_all), jnp.stack(grad_g_all), jnp.stack(grad_q_all), jnp.stack(grad_o_all), jnp.stack(grad_kv_all), feat_total)
```

```python
import jax
import jax.numpy as jnp
from jax import lax
from jax.experimental import pallas as pl
from jax.experimental.pallas import tpu as pltpu
from jax.sharding import PartitionSpec as P

MESH = pl.DeviceIdType.MESH
F32 = jnp.float32
BF16 = jnp.bfloat16
TOK = 256
D = 8192
HALF = D // 2
CHUNK = 1024
HD = 128
VCOLS = 240
SCALE = HD ** (-0.5)
NSEM = 96

NT = (((1,), (1,)), ((), ()))
TN = (((0,), (0,)), ((), ()))


def dot(a, b, dims=(((1,), (0,)), ((), ()))):
    return lax.dot_general(a, b, dims, preferred_element_type=F32)


class Links:
    def __init__(self, send_sems, recv_sems):
        self.s = lax.axis_index("section")
        index = lax.axis_index("mp")
        self.z, self.x, self.y = index // 8, (index // 4) % 2, index % 4
        self.send_sems, self.recv_sems = send_sems, recv_sems
        self.copies = []

    def coord(self, axis, d):
        if axis == "x":
            return (self.x + d) % 2
        return (getattr(self, axis) + d) % 4

    def peer(self, axis, d):
        at = {"s": self.s, "z": self.z, "x": self.x, "y": self.y}
        at[axis] = self.coord(axis, d)
        return (at["s"], at["z"] * 8 + at["x"] * 4 + at["y"])

    def barrier(self):
        sem = pltpu.get_barrier_semaphore()
        peers = [(a, d) for a in ("z", "y", "s") for d in (1, 2, 3)] + [("x", 1)]
        for a, d in peers:
            pl.semaphore_signal(sem, inc=1, device_id=self.peer(a, d), device_id_type=MESH)
        pl.semaphore_wait(sem, len(peers))

    def send(self, axis, d, src, dst):
        at = len(self.copies)
        copy = pltpu.make_async_remote_copy(
            src_ref=src,
            dst_ref=dst,
            send_sem=self.send_sems.at[at],
            recv_sem=self.recv_sems.at[at],
            device_id=self.peer(axis, d),
            device_id_type=MESH,
        )
        copy.start()
        self.copies.append(copy)
        return copy

    def ring(self, axis, src, dst):
        return [self.send(axis, d, src(d), dst(d)) for d in (1, 3, 2)]

    def finish(self):
        for copy in self.copies:
            copy.wait_send()


def arrive(copies):
    for copy in copies:
        copy.wait_recv()


def columns(start, stop, body, step=CHUNK):
    @pl.loop(0, (stop - start) // step)
    def _(i):
        body(pl.ds(pl.multiple_of(start + i * step, step), step))


def layer_kernel(
    tok_ref, cot_ref, gain_ref, vis_ref, feat_ref, wq_hbm, wo_hbm, wkv_hbm,
    n_out, c_out, attn_out, dq_out, gkv_out, gx_out, gg_out, gi_out,
    n_all, c_all, wq, wo, wkv,
    fold_n, fold_c, from_n, from_c,
    pk, pv, k1, v1, ks1, vs1, k2, v2, ks2, vs2, kx, vx, keys, values,
    dk, dv, rk, rv, dkg, dvg,
    pd, da1, db1, sa1, sb1, da2, db2, own_d, fold_d, from_d,
    df, dfr, img_s, img_z, img_x, gz, gy, gx2,
    send_sems, recv_sems, local_sems,
):
    net = Links(send_sems, recv_sems)
    s, z, x, y = net.s, net.z, net.x, net.y
    loads = []
    wkv[VCOLS:, :] = jnp.zeros((256 - VCOLS, 2048), BF16)
    for i, (src, dst) in enumerate(((wkv_hbm, wkv.at[:VCOLS]), (wq_hbm, wq), (wo_hbm, wo))):
        copy = pltpu.make_async_copy(src, dst, local_sems.at[i])
        copy.start()
        loads.append(copy)
    net.barrier()

    xf = tok_ref[...].astype(F32)
    rinv = lax.rsqrt(jnp.mean(xf * xf, axis=-1, keepdims=True) + 1e-05)

    def normed_at(cols):
        return tok_ref[:, cols].astype(F32) * rinv * gain_ref[:, cols]

    def fold_step(i):
        lo = pl.ds(pl.multiple_of(i * CHUNK, CHUNK), CHUNK)
        hi = pl.ds(pl.multiple_of(HALF + i * CHUNK, CHUNK), CHUNK)
        fold_n[:, lo] = jnp.concatenate([normed_at(lo), normed_at(hi)], axis=0).astype(BF16)
        fold_c[:, lo] = jnp.concatenate(
            [cot_ref[:, lo].astype(F32), cot_ref[:, hi].astype(F32)], axis=0
        ).astype(BF16)

    pl.loop(0, HALF // CHUNK)(fold_step)
    x_n = net.send("x", 1, fold_n, from_n)
    x_c = net.send("x", 1, fold_c, from_c)

    loads[0].wait()

    def kv_step(h):
        cols = pl.ds(pl.multiple_of(h * HD, HD), HD)
        vcols = pl.ds(pl.multiple_of(1024 + h * HD, HD), HD)
        feats = feat_ref[...]
        pk[h // 2, h % 2] = dot(feats, wkv[:, cols]).reshape(4, 128, HD)
        pv[h // 2, h % 2] = dot(feats, wkv[:, vcols]).astype(BF16).reshape(4, 128, HD)

    pl.loop(0, 8)(kv_step)
    k_1 = net.ring("y", lambda d: pk.at[:, :, net.coord("y", d)], lambda d: k1.at[d - 1])
    v_1 = net.ring("z", lambda d: pv.at[net.coord("z", d)], lambda d: v1.at[d - 1])

    def unfold(folded, received, full):
        def step(i):
            lo = pl.ds(pl.multiple_of(i * CHUNK, CHUNK), CHUNK)
            hi = pl.ds(pl.multiple_of(HALF + i * CHUNK, CHUNK), CHUNK)
            mine = folded[:, lo].astype(F32)
            other = received[:, lo].astype(F32)
            for at, cols in ((0, lo), (8, hi)):
                a, b = mine[at : at + 8], other[at : at + 8]
                first = jnp.where(x == 0, a, b)
                second = jnp.where(x == 0, b, a)
                full[z, y, :, cols] = jnp.concatenate([first, second], axis=0).astype(BF16)

        pl.loop(0, HALF // CHUNK)(step)

    a_cols, b_cols = pl.ds(0, HALF), pl.ds(HALF, HALF)

    def gather_start(full):
        own_a, own_b = full.at[z, y, :, a_cols], full.at[z, y, :, b_cols]
        za = net.ring("z", lambda d: own_a, lambda d: own_a)
        yb = net.ring("y", lambda d: own_b, lambda d: own_b)
        return za, yb

    def gather_on(full, za, yb):
        arrive(za)
        part = full.at[:, y, :, a_cols]
        out = net.ring("y", lambda d: part, lambda d: part)
        arrive(yb)
        part_b = full.at[z, :, :, b_cols]
        return out + net.ring("z", lambda d: part_b, lambda d: part_b)

    x_n.wait_recv()
    unfold(fold_n, from_n, n_all)
    n_1 = gather_start(n_all)

    arrive(k_1)
    for a in range(4):
        for b in range(2):
            total = pk[a, b, y]
            for d in range(3):
                total += k1[d, a, b]
            ks1[a, b] = total
    k_2 = net.ring("z", lambda d: ks1.at[net.coord("z", d)], lambda d: k2.at[d - 1])
    arrive(v_1)
    for b in range(2):
        for c in range(4):
            total = pv[z, b, c].astype(F32)
            for d in range(3):
                total += v1[d, b, c].astype(F32)
            vs1[b, c] = total.astype(BF16)
    v_2 = net.ring("y", lambda d: vs1.at[:, net.coord("y", d)], lambda d: v2.at[d - 1])

    n_2 = gather_on(n_all, *n_1)
    x_c.wait_recv()
    unfold(fold_c, from_c, c_all)

    arrive(k_2)
    arrive(v_2)
    for b in range(2):
        total = ks1[z, b]
        vtotal = vs1[b, y].astype(F32)
        for d in range(3):
            total += k2[d, b]
            vtotal += v2[d, b].astype(F32)
        ks2[b] = total
        vs2[b] = vtotal.astype(BF16)
    k_x = net.send("x", 1, ks2.at[1 - x], kx)
    v_x = net.send("x", 1, vs2.at[1 - x], vx)
    c_1 = gather_start(c_all)
    k_x.wait_recv()
    v_x.wait_recv()
    keys[y] = (ks2[x] + kx[...]).astype(BF16)
    values[y] = (vs2[x].astype(F32) + vx[...].astype(F32)).astype(BF16)
    k_3 = net.ring("y", lambda d: keys.at[y], lambda d: keys.at[y])
    v_3 = net.ring("y", lambda d: values.at[y], lambda d: values.at[y])

    arrive(n_2)
    stores = []
    copy = pltpu.make_async_copy(n_all, n_out, local_sems.at[3])
    copy.start()
    stores.append(copy)
    c_2 = gather_on(c_all, *c_1)

    loads[1].wait()

    def query_step(i, acc):
        cols = pl.ds(pl.multiple_of(i * CHUNK, CHUNK), CHUNK)
        return acc + dot(n_all[:, :, :, cols].reshape(TOK, CHUNK), wq[cols, :])

    query = lax.fori_loop(0, D // CHUNK, query_step, jnp.zeros((TOK, 256), F32)).astype(BF16)

    arrive(k_3)
    arrive(v_3)
    key = keys[...].reshape(512, HD)
    value = values[...].reshape(512, HD)
    image_of = lax.broadcasted_iota(jnp.int32, (TOK, 512), 1) // 128
    late = lax.broadcasted_iota(jnp.int32, (TOK, 512), 0) >= 128
    allowed = image_of < jnp.where(late, vis_ref[1], vis_ref[0])
    probs, weights = [], []
    for j in range(2):
        q = query[:, j * HD : (j + 1) * HD]
        scores = jnp.where(allowed, dot(q, key, NT) * SCALE, -1e30)
        expo = jnp.exp(scores - jnp.max(scores, axis=-1, keepdims=True))
        prob = expo / jnp.sum(expo, axis=-1, keepdims=True)
        probs.append(prob)
        weights.append(prob.astype(BF16))
        attn_out[:, j * HD : (j + 1) * HD] = dot(weights[j], value).astype(BF16)

    arrive(c_2)
    copy = pltpu.make_async_copy(c_all, c_out, local_sems.at[4])
    copy.start()
    stores.append(copy)
    loads[2].wait()

    def d_attn_step(i, acc):
        cols = pl.ds(pl.multiple_of(i * CHUNK, CHUNK), CHUNK)
        return acc + dot(c_all[:, :, :, cols].reshape(TOK, CHUNK), wo[:, cols], NT)

    d_attn = lax.fori_loop(0, D // CHUNK, d_attn_step, jnp.zeros((TOK, 256), F32)).astype(BF16)
    d_key = jnp.zeros((512, HD), F32)
    d_value = jnp.zeros((512, HD), F32)
    for j in range(2):
        heads = slice(j * HD, (j + 1) * HD)
        da = d_attn[:, heads]
        d_prob = dot(da, value, NT)
        delta = jnp.sum(probs[j] * d_prob, axis=-1, keepdims=True)
        d_score = (probs[j] * (d_prob - delta) * SCALE).astype(BF16)
        dq_out[:, heads] = dot(d_score, key).astype(BF16)
        d_key += dot(d_score, query[:, heads], TN)
        d_value += dot(weights[j], da, TN)
    dk[...] = d_key.astype(BF16).reshape(4, 128, HD)
    dv[...] = d_value.astype(BF16).reshape(4, 128, HD)
    dk_1 = net.ring("y", lambda d: dk.at[net.coord("y", d)], lambda d: rk.at[d - 1])
    dv_1 = net.ring("y", lambda d: dv.at[net.coord("y", d)], lambda d: rv.at[d - 1])

    def d_normed_step(cols):
        part = dot(dq_out[...], wq[cols, :], NT)
        pd[:, :, :, cols] = part.astype(BF16).reshape(4, 4, 16, CHUNK)

    columns(0, HALF, d_normed_step)
    da_1 = net.ring(
        "y", lambda d: pd.at[:, net.coord("y", d), :, a_cols], lambda d: da1.at[d - 1]
    )
    columns(HALF, D, d_normed_step)
    db_1 = net.ring("z", lambda d: pd.at[net.coord("z", d), :, :, b_cols], lambda d: db1.at[d - 1])

    arrive(dk_1)
    arrive(dv_1)
    total = dk[y].astype(F32)
    vtotal = dv[y].astype(F32)
    for d in range(3):
        total += rk[d].astype(F32)
        vtotal += rv[d].astype(F32)
    dkg[z, x, y] = total.astype(BF16)
    dvg[z, x, y] = vtotal.astype(BF16)
    mine_k, mine_v = dkg.at[z, x, y], dvg.at[z, x, y]
    dk_2 = net.send("x", 1, mine_k, mine_k)
    dv_2 = net.send("x", 1, mine_v, mine_v)
    dk_2.wait_recv()
    dv_2.wait_recv()
    pair_k, pair_v = dkg.at[z, :, y], dvg.at[z, :, y]
    dk_3 = net.ring("z", lambda d: pair_k, lambda d: pair_k)
    dv_3 = net.ring("y", lambda d: pair_v, lambda d: pair_v)
    arrive(dk_3)
    line_k = dkg.at[:, :, y]
    dk_4 = net.ring("y", lambda d: line_k, lambda d: line_k)
    arrive(dv_3)
    line_v = dvg.at[z]
    dv_4 = net.ring("z", lambda d: line_v, lambda d: line_v)

    arrive(da_1)

    def sum_a(i):
        cols = pl.ds(pl.multiple_of(i * CHUNK, CHUNK), CHUNK)
        total = pd[:, y, :, cols].astype(F32)
        for d in range(3):
            total += da1[d, :, :, cols].astype(F32)
        sa1[:, :, cols] = total.astype(BF16)

    pl.loop(0, HALF // CHUNK)(sum_a)
    da_2 = net.ring("z", lambda d: sa1.at[net.coord("z", d)], lambda d: da2.at[d - 1])
    arrive(db_1)

    def sum_b(i):
        cols = pl.ds(pl.multiple_of(i * CHUNK, CHUNK), CHUNK)
        far = pl.ds(pl.multiple_of(HALF + i * CHUNK, CHUNK), CHUNK)
        total = pd[z, :, :, far].astype(F32)
        for d in range(3):
            total += db1[d, :, :, cols].astype(F32)
        sb1[:, :, cols] = total.astype(BF16)

    pl.loop(0, HALF // CHUNK)(sum_b)
    db_2 = net.ring("y", lambda d: sb1.at[net.coord("y", d)], lambda d: db2.at[d - 1])

    arrive(dk_4)
    arrive(dv_4)
    feats = feat_ref[...]
    d_feats = jnp.zeros((512, 256), F32)
    for h in range(8):
        for at, full in ((h * HD, dkg), (1024 + h * HD, dvg)):
            grad = full[h // 2, h % 2].reshape(512, HD)
            gkv_out[:, at : at + HD] = dot(feats, grad, TN).astype(BF16)
            d_feats += dot(grad, wkv[:, at : at + HD], NT)
    df[...] = d_feats.reshape(4, 128, 256)
    f_1 = net.ring("s", lambda d: df.at[net.coord("s", d)], lambda d: dfr.at[d - 1])

    arrive(da_2)
    arrive(db_2)

    def sum_ab(i):
        cols = pl.ds(pl.multiple_of(i * CHUNK, CHUNK), CHUNK)
        ta = sa1[z, :, cols].astype(F32)
        tb = sb1[y, :, cols].astype(F32)
        for d in range(3):
            ta += da2[d, :, cols].astype(F32)
            tb += db2[d, :, cols].astype(F32)
        own_d[:8, cols] = jnp.where(x == 0, ta[:8], ta[8:])
        own_d[8:, cols] = jnp.where(x == 0, tb[:8], tb[8:])
        fold_d[:, cols] = jnp.concatenate(
            [jnp.where(x == 0, ta[8:], ta[:8]), jnp.where(x == 0, tb[8:], tb[:8])], axis=0
        ).astype(BF16)

    pl.loop(0, HALF // CHUNK)(sum_ab)
    d_x = net.send("x", 1, fold_d, from_d)

    arrive(f_1)
    img = df[s]
    for d in range(3):
        img += dfr[d]
    img_s[...] = img.reshape(4, 32, 256)
    img_z[z] = img_s[z]
    f_2 = net.ring("z", lambda d: img_s.at[net.coord("z", d)], lambda d: img_z.at[z])

    d_x.wait_recv()
    both = own_d[...] + from_d[...].astype(F32)
    dn = jnp.concatenate([both[:8], both[8:]], axis=1)
    xf = tok_ref[...].astype(F32)
    scaled = dn * gain_ref[...]
    gx_out[...] = (
        rinv * scaled - xf * rinv * rinv * rinv * jnp.mean(xf * scaled, axis=-1, keepdims=True)
    ).astype(BF16)
    gain = jnp.sum(dn * xf * rinv, axis=0, keepdims=True)
    for i in range(8):
        gz[z, i : i + 1, :] = gain[:, i * 1024 : (i + 1) * 1024]
    g_1 = net.ring("z", lambda d: gz.at[z], lambda d: gz.at[z])

    arrive(f_2)
    img_x[x] = img_z[:, pl.ds(pl.multiple_of(x * 16, 16), 16), :]
    far = pl.ds(pl.multiple_of((1 - x) * 16, 16), 16)
    f_3 = net.send("x", 1, img_z.at[:, far], img_x.at[x])
    arrive(g_1)
    gy[y] = (gz[0] + gz[1]) + (gz[2] + gz[3])
    g_2 = net.ring("y", lambda d: gy.at[y], lambda d: gy.at[y])
    f_3.wait_recv()

    def tile(d):
        return pl.ds(pl.multiple_of((net.coord("y", d) // 2) * 8, 8), 8)

    gi_out[y] = img_x[:, :, tile(0), :]
    f_4 = net.ring("y", lambda d: img_x.at[:, :, tile(d)], lambda d: gi_out.at[y])
    arrive(g_2)
    gx2[x] = (gy[0] + gy[1]) + (gy[2] + gy[3])
    g_3 = net.send("x", 1, gx2.at[x], gx2.at[x])
    g_3.wait_recv()
    gg_out[...] = gx2[0] + gx2[1]
    arrive(f_4)
    for copy in stores:
        copy.wait()
    net.finish()


def run_layer(tokens, cotangent, gain_row, visible, feats, w_q, w_o, w_kv):
    any_spec = pl.BlockSpec(memory_space=pl.ANY)
    vmem = pl.BlockSpec(memory_space=pltpu.VMEM)
    smem = pl.BlockSpec(memory_space=pltpu.SMEM)
    shape = jax.ShapeDtypeStruct
    b, f = (lambda *dims: pltpu.VMEM(dims, BF16)), (lambda *dims: pltpu.VMEM(dims, F32))
    return pl.pallas_call(
        layer_kernel,
        out_shape=(
            shape((4, 4, 16, D), BF16),
            shape((4, 4, 16, D), BF16),
            shape((TOK, 256), BF16),
            shape((TOK, 256), BF16),
            shape((256, 2048), BF16),
            shape((8, D), BF16),
            shape((8, 1024), F32),
            shape((4, 2, 4, 8, 256), F32),
        ),
        in_specs=[vmem, vmem, vmem, smem, vmem, any_spec, any_spec, any_spec],
        out_specs=(any_spec, any_spec, vmem, vmem, vmem, vmem, vmem, vmem),
        scratch_shapes=[
            b(4, 4, 16, D), b(4, 4, 16, D), b(D, 256), b(256, D), b(256, 2048),
            b(16, HALF), b(16, HALF), b(16, HALF), b(16, HALF),
            f(4, 2, 4, 128, HD), b(4, 2, 4, 128, HD),
            f(3, 4, 2, 128, HD), b(3, 2, 4, 128, HD),
            f(4, 2, 128, HD), b(2, 4, 128, HD),
            f(3, 2, 128, HD), b(3, 2, 128, HD),
            f(2, 128, HD), b(2, 128, HD),
            f(128, HD), b(128, HD),
            b(4, 128, HD), b(4, 128, HD),
            b(4, 128, HD), b(4, 128, HD), b(3, 128, HD), b(3, 128, HD),
            b(4, 2, 4, 128, HD), b(4, 2, 4, 128, HD),
            b(4, 4, 16, D),
            b(3, 4, 16, HALF), b(3, 4, 16, HALF),
            b(4, 16, HALF), b(4, 16, HALF),
            b(3, 16, HALF), b(3, 16, HALF),
            f(16, HALF), b(16, HALF), b(16, HALF),
            f(4, 128, 256), f(3, 128, 256),
            f(4, 32, 256), f(4, 32, 256), f(2, 4, 16, 256),
            f(4, 8, 1024), f(4, 8, 1024), f(2, 8, 1024),
            pltpu.SemaphoreType.DMA((NSEM,)),
            pltpu.SemaphoreType.DMA((NSEM,)),
            pltpu.SemaphoreType.DMA((5,)),
        ],
        compiler_params=pltpu.CompilerParams(
            collective_id=0, has_side_effects=True, vmem_limit_bytes=58 * 1024 * 1024
        ),
        cost_estimate=pl.CostEstimate(
            flops=6 * 10**9, bytes_accessed=20 * 2**20, transcendentals=2 * 256 * 512
        ),
        name="layer",
    )(tokens, cotangent, gain_row, visible, feats, w_q, w_o, w_kv)


def per_device(tokens, upstream, norm_gain, w_query, w_output, w_keyvalue, image_feats, visible):
    wide_rows = lax.all_gather(image_feats, "section", axis=0, tiled=True)
    mixed = lax.all_to_all(wide_rows, "mp", split_axis=1, concat_axis=0, tiled=True)
    feats = mixed.reshape(32, 4, 4, VCOLS).transpose(1, 0, 2, 3).reshape(512, VCOLS)
    feats = jnp.pad(feats, ((0, 0), (0, 256 - VCOLS)))
    normed, cotangent, attn, d_query, grad_kv, grad_x, grad_g, image = run_layer(
        tokens[0], upstream[0], norm_gain, visible, feats, w_query[0], w_output[0], w_keyvalue[0]
    )
    grad_q = lax.dot_general(normed.reshape(TOK, D), d_query, TN, preferred_element_type=F32)
    grad_out = lax.dot_general(attn, cotangent.reshape(TOK, D), TN, preferred_element_type=F32)
    odd = lax.axis_index("mp") % 2
    rows = lax.dynamic_slice_in_dim(image, odd * 4, 4, 3)[..., :VCOLS]
    grad_image = rows.transpose(3, 2, 1, 0, 4).reshape(4, 32 * VCOLS)
    return (
        grad_x[None],
        grad_g.reshape(1, D),
        grad_q.astype(BF16)[None],
        grad_out.astype(BF16)[None],
        grad_kv[None, :VCOLS],
        grad_image,
    )


def solution(mesh):
    placed = (
        P("section", "mp", None),
        P("section", "mp", None),
        P("section", None),
        P("section", None, "mp"),
        P("section", "mp", None),
        P("section", "mp", None),
        P(("section", "mp"), None),
        P(),
    )
    return jax.shard_map(
        per_device,
        mesh=mesh,
        in_specs=placed,
        out_specs=(
            P("section", "mp", None),
            P("section", None),
            P("section", None, "mp"),
            P("section", "mp", None),
            P("section", "mp", None),
            P(("section", "mp"), None),
        ),
        check_vma=False,
    )
```

```python
import jax
import jax.numpy as jnp
from jax import lax
from jax.experimental import pallas as pl
from jax.experimental.pallas import tpu as pltpu
from jax.sharding import PartitionSpec as P

MESH = pl.DeviceIdType.MESH
F32 = jnp.float32
BF16 = jnp.bfloat16
TOK = 256
D = 8192
HALF = D // 2
CHUNK = 1024
HD = 128
VCOLS = 240
SCALE = HD ** (-0.5)
NSEM = 128

NT = (((1,), (1,)), ((), ()))
TN = (((0,), (0,)), ((), ()))


def dot(a, b, dims=(((1,), (0,)), ((), ()))):
    return lax.dot_general(a, b, dims, preferred_element_type=F32)


class Links:
    def __init__(self, send_sems, recv_sems):
        self.s = lax.axis_index("section")
        index = lax.axis_index("mp")
        self.z, self.x, self.y = index // 8, (index // 4) % 2, index % 4
        self.send_sems, self.recv_sems = send_sems, recv_sems
        self.copies = []

    def coord(self, axis, d):
        if axis == "x":
            return (self.x + d) % 2
        return (getattr(self, axis) + d) % 4

    def peer(self, axis, d):
        at = {"s": self.s, "z": self.z, "x": self.x, "y": self.y}
        at[axis] = self.coord(axis, d)
        return (at["s"], at["z"] * 8 + at["x"] * 4 + at["y"])

    def barrier(self):
        sem = pltpu.get_barrier_semaphore()
        peers = [(a, d) for a in ("z", "y", "s") for d in (1, 2, 3)] + [("x", 1)]
        for a, d in peers:
            pl.semaphore_signal(sem, inc=1, device_id=self.peer(a, d), device_id_type=MESH)
        pl.semaphore_wait(sem, len(peers))

    def send(self, axis, d, src, dst):
        at = len(self.copies)
        copy = pltpu.make_async_remote_copy(
            src_ref=src,
            dst_ref=dst,
            send_sem=self.send_sems.at[at],
            recv_sem=self.recv_sems.at[at],
            device_id=self.peer(axis, d),
            device_id_type=MESH,
        )
        copy.start()
        self.copies.append(copy)
        return copy

    def ring(self, axis, src, dst):
        return [self.send(axis, d, src(d), dst(d)) for d in (1, 3, 2)]

    def finish(self):
        for copy in self.copies:
            copy.wait_send()


def arrive(copies):
    for copy in copies:
        copy.wait_recv()


def columns(start, stop, body, step=CHUNK):
    @pl.loop(0, (stop - start) // step)
    def _(i):
        body(pl.ds(pl.multiple_of(start + i * step, step), step))


def layer_kernel(
    tok_ref, cot_ref, gain_ref, vis_ref, unit_ref, wq_hbm, wo_hbm, wkv_hbm,
    n_out, c_out, attn_out, dq_out, gkv_out, gx_out, gg_out, gi_out,
    n_all, c_all, wq, wo, wkv,
    u_y, u_z, u_x, feat_all,
    fold_n, fold_c, from_n, from_c,
    pk, pv, k1, v1, ks1, vs1, k2, v2, ks2, vs2, kx, vx, keys, values,
    dk, dv, rk, rv, dkg, dvg,
    pd, da1, db1, sa1, sb1, da2, db2, own_d, fold_d, from_d,
    df, dfr, img_s, img_z, img_x, gi_all, gain_part, gz, gy, gx2,
    send_sems, recv_sems, local_sems,
):
    net = Links(send_sems, recv_sems)
    s, z, x, y = net.s, net.z, net.x, net.y
    loads = []
    wkv[VCOLS:, :] = jnp.zeros((256 - VCOLS, 2048), BF16)
    for i, (src, dst) in enumerate(((wkv_hbm, wkv.at[:VCOLS]), (wq_hbm, wq), (wo_hbm, wo))):
        copy = pltpu.make_async_copy(src, dst, local_sems.at[i])
        copy.start()
        loads.append(copy)
    net.barrier()

    u_y[y] = unit_ref[:, :, y]
    u_1 = net.ring("y", lambda d: unit_ref.at[:, :, net.coord("y", d)], lambda d: u_y.at[y])

    xf = tok_ref[...].astype(F32)
    rinv = lax.rsqrt(jnp.mean(xf * xf, axis=-1, keepdims=True) + 1e-05)

    def normed_at(cols):
        return tok_ref[:, cols].astype(F32) * rinv * gain_ref[:, cols]

    def fold_step(i):
        lo = pl.ds(pl.multiple_of(i * CHUNK, CHUNK), CHUNK)
        hi = pl.ds(pl.multiple_of(HALF + i * CHUNK, CHUNK), CHUNK)
        fold_n[:, lo] = jnp.concatenate([normed_at(lo), normed_at(hi)], axis=0).astype(BF16)
        fold_c[:, lo] = jnp.concatenate(
            [cot_ref[:, lo].astype(F32), cot_ref[:, hi].astype(F32)], axis=0
        ).astype(BF16)

    pl.loop(0, HALF // CHUNK)(fold_step)
    x_n = net.send("x", 1, fold_n, from_n)
    arrive(u_1)
    u_z[z] = u_y[:, z]
    u_2 = net.ring("z", lambda d: u_y.at[:, net.coord("z", d)], lambda d: u_z.at[z])
    x_c = net.send("x", 1, fold_c, from_c)

    def unfold(folded, received, full):
        def step(i):
            lo = pl.ds(pl.multiple_of(i * CHUNK, CHUNK), CHUNK)
            hi = pl.ds(pl.multiple_of(HALF + i * CHUNK, CHUNK), CHUNK)
            mine = folded[:, lo].astype(F32)
            other = received[:, lo].astype(F32)
            for at, cols in ((0, lo), (8, hi)):
                a, b = mine[at : at + 8], other[at : at + 8]
                first = jnp.where(x == 0, a, b)
                second = jnp.where(x == 0, b, a)
                full[z, y, :, cols] = jnp.concatenate([first, second], axis=0).astype(BF16)

        pl.loop(0, HALF // CHUNK)(step)

    a_cols, b_cols = pl.ds(0, HALF), pl.ds(HALF, HALF)

    def gather_start(full):
        own_a, own_b = full.at[z, y, :, a_cols], full.at[z, y, :, b_cols]
        za = net.ring("z", lambda d: own_a, lambda d: own_a)
        yb = net.ring("y", lambda d: own_b, lambda d: own_b)
        return za, yb

    def gather_on(full, za, yb):
        arrive(za)
        part = full.at[:, y, :, a_cols]
        out = net.ring("y", lambda d: part, lambda d: part)
        arrive(yb)
        part_b = full.at[z, :, :, b_cols]
        return out + net.ring("z", lambda d: part_b, lambda d: part_b)


    arrive(u_2)
    u_x[x] = u_z[:, :, x]
    u_3 = net.send("x", 1, u_z.at[:, :, 1 - x], u_x.at[x])
    x_n.wait_recv()
    unfold(fold_n, from_n, n_all)
    n_1 = gather_start(n_all)

    u_3.wait_recv()
    units = u_x[...].reshape(256, HD).astype(BF16)
    row = lax.broadcasted_iota(jnp.int32, (128, 256), 0)
    col = lax.broadcasted_iota(jnp.int32, (128, 256), 1)
    at = (((row // 16) % 2 * 4 + row // 32) * 4 + (row // 4) % 4) * 8 + row % 4
    for half in range(2):
        pick = jnp.where(col == at + 4 * half, 1.0, 0.0).astype(BF16)
        feat_all[s, :, half * HD : (half + 1) * HD] = dot(pick, units).astype(BF16)
    f_0 = net.ring("s", lambda d: feat_all.at[s], lambda d: feat_all.at[s])
    arrive(f_0)

    loads[0].wait()

    def kv_step(h):
        cols = pl.ds(pl.multiple_of(h * HD, HD), HD)
        vcols = pl.ds(pl.multiple_of(1024 + h * HD, HD), HD)
        feats = feat_all[...].reshape(512, 256)
        pk[h // 2, h % 2] = dot(feats, wkv[:, cols]).astype(BF16).reshape(4, 128, HD)
        pv[h // 2, h % 2] = dot(feats, wkv[:, vcols]).astype(BF16).reshape(4, 128, HD)

    pl.loop(0, 8)(kv_step)
    k_1 = net.ring("y", lambda d: pk.at[:, :, net.coord("y", d)], lambda d: k1.at[d - 1])
    v_1 = net.ring("z", lambda d: pv.at[net.coord("z", d)], lambda d: v1.at[d - 1])

    arrive(k_1)
    for a in range(4):
        for b in range(2):
            total = pk[a, b, y].astype(F32)
            for d in range(3):
                total += k1[d, a, b].astype(F32)
            ks1[a, b] = total
    k_2 = net.ring("z", lambda d: ks1.at[net.coord("z", d)], lambda d: k2.at[d - 1])
    arrive(v_1)
    for b in range(2):
        for c in range(4):
            total = pv[z, b, c].astype(F32)
            for d in range(3):
                total += v1[d, b, c].astype(F32)
            vs1[b, c] = total
    v_2 = net.ring("y", lambda d: vs1.at[:, net.coord("y", d)], lambda d: v2.at[d - 1])

    n_2 = gather_on(n_all, *n_1)
    x_c.wait_recv()
    unfold(fold_c, from_c, c_all)

    arrive(k_2)
    arrive(v_2)
    for b in range(2):
        total = ks1[z, b]
        vtotal = vs1[b, y]
        for d in range(3):
            total += k2[d, b]
            vtotal += v2[d, b]
        ks2[b] = total
        vs2[b] = vtotal
    k_x = net.send("x", 1, ks2.at[1 - x], kx)
    v_x = net.send("x", 1, vs2.at[1 - x], vx)
    c_1 = gather_start(c_all)
    k_x.wait_recv()
    v_x.wait_recv()
    keys[y] = (ks2[x] + kx[...]).astype(BF16)
    values[y] = (vs2[x] + vx[...]).astype(BF16)
    k_3 = net.ring("y", lambda d: keys.at[y], lambda d: keys.at[y])
    v_3 = net.ring("y", lambda d: values.at[y], lambda d: values.at[y])

    arrive(n_2)
    stores = []
    copy = pltpu.make_async_copy(n_all, n_out, local_sems.at[3])
    copy.start()
    stores.append(copy)
    c_2 = gather_on(c_all, *c_1)

    loads[1].wait()

    def query_step(i, acc):
        cols = pl.ds(pl.multiple_of(i * CHUNK, CHUNK), CHUNK)
        return acc + dot(n_all[:, :, :, cols].reshape(TOK, CHUNK), wq[cols, :])

    query = lax.fori_loop(0, D // CHUNK, query_step, jnp.zeros((TOK, 256), F32)).astype(BF16)

    arrive(k_3)
    arrive(v_3)
    key = keys[...].reshape(512, HD)
    value = values[...].reshape(512, HD)
    image_of = lax.broadcasted_iota(jnp.int32, (TOK, 512), 1) // 128
    late = lax.broadcasted_iota(jnp.int32, (TOK, 512), 0) >= 128
    allowed = image_of < jnp.where(late, vis_ref[1], vis_ref[0])
    probs, weights = [], []
    for j in range(2):
        q = query[:, j * HD : (j + 1) * HD]
        scores = jnp.where(allowed, dot(q, key, NT) * SCALE, -1e30)
        expo = jnp.exp(scores - jnp.max(scores, axis=-1, keepdims=True))
        prob = expo / jnp.sum(expo, axis=-1, keepdims=True)
        probs.append(prob)
        weights.append(prob.astype(BF16))
        attn_out[:, j * HD : (j + 1) * HD] = dot(weights[j], value).astype(BF16)

    arrive(c_2)
    copy = pltpu.make_async_copy(c_all, c_out, local_sems.at[4])
    copy.start()
    stores.append(copy)
    loads[2].wait()

    def d_attn_step(i, acc):
        cols = pl.ds(pl.multiple_of(i * CHUNK, CHUNK), CHUNK)
        return acc + dot(c_all[:, :, :, cols].reshape(TOK, CHUNK), wo[:, cols], NT)

    d_attn = lax.fori_loop(0, D // CHUNK, d_attn_step, jnp.zeros((TOK, 256), F32)).astype(BF16)
    d_key = jnp.zeros((512, HD), F32)
    d_value = jnp.zeros((512, HD), F32)
    for j in range(2):
        heads = slice(j * HD, (j + 1) * HD)
        da = d_attn[:, heads]
        d_prob = dot(da, value, NT)
        delta = jnp.sum(probs[j] * d_prob, axis=-1, keepdims=True)
        d_score = (probs[j] * (d_prob - delta) * SCALE).astype(BF16)
        dq_out[:, heads] = dot(d_score, key).astype(BF16)
        d_key += dot(d_score, query[:, heads], TN)
        d_value += dot(weights[j], da, TN)
    dk[...] = d_key.astype(BF16).reshape(4, 128, HD)
    dv[...] = d_value.astype(BF16).reshape(4, 128, HD)
    dk_1 = net.ring("y", lambda d: dk.at[net.coord("y", d)], lambda d: rk.at[d - 1])
    dv_1 = net.ring("y", lambda d: dv.at[net.coord("y", d)], lambda d: rv.at[d - 1])

    def d_normed_step(cols):
        part = dot(dq_out[...], wq[cols, :], NT)
        pd[:, :, :, cols] = part.astype(BF16).reshape(4, 4, 16, CHUNK)
        normed = n_all[:, :, :, cols].reshape(TOK, CHUNK).astype(F32)
        gain_part[:, cols] = jnp.sum(part * normed, axis=0, keepdims=True) / gain_ref[:, cols]

    columns(0, HALF, d_normed_step)
    da_1 = net.ring(
        "y", lambda d: pd.at[:, net.coord("y", d), :, a_cols], lambda d: da1.at[d - 1]
    )
    columns(HALF, D, d_normed_step)
    db_1 = net.ring("z", lambda d: pd.at[net.coord("z", d), :, :, b_cols], lambda d: db1.at[d - 1])
    for i in range(8):
        gz[z, i : i + 1, :] = gain_part[:, i * 1024 : (i + 1) * 1024]
    g_1 = net.ring("z", lambda d: gz.at[z], lambda d: gz.at[z])

    arrive(dk_1)
    arrive(dv_1)
    total = dk[y].astype(F32)
    vtotal = dv[y].astype(F32)
    for d in range(3):
        total += rk[d].astype(F32)
        vtotal += rv[d].astype(F32)
    dkg[z, x, y] = total.astype(BF16)
    dvg[z, x, y] = vtotal.astype(BF16)
    mine_k, mine_v = dkg.at[z, x, y], dvg.at[z, x, y]
    dk_2 = net.send("x", 1, mine_k, mine_k)
    dv_2 = net.send("x", 1, mine_v, mine_v)
    dk_2.wait_recv()
    dv_2.wait_recv()
    pair_k, pair_v = dkg.at[z, :, y], dvg.at[z, :, y]
    dk_3 = net.ring("z", lambda d: pair_k, lambda d: pair_k)
    dv_3 = net.ring("y", lambda d: pair_v, lambda d: pair_v)
    arrive(g_1)
    gy[y] = (gz[0] + gz[1]) + (gz[2] + gz[3])
    g_2 = net.ring("y", lambda d: gy.at[y], lambda d: gy.at[y])
    arrive(dk_3)
    line_k = dkg.at[:, :, y]
    dk_4 = net.ring("y", lambda d: line_k, lambda d: line_k)
    arrive(dv_3)
    line_v = dvg.at[z]
    dv_4 = net.ring("z", lambda d: line_v, lambda d: line_v)

    arrive(g_2)
    gx2[x] = (gy[0] + gy[1]) + (gy[2] + gy[3])
    g_3 = net.send("x", 1, gx2.at[x], gx2.at[x])
    arrive(da_1)

    def sum_a(i):
        cols = pl.ds(pl.multiple_of(i * CHUNK, CHUNK), CHUNK)
        total = pd[:, y, :, cols].astype(F32)
        for d in range(3):
            total += da1[d, :, :, cols].astype(F32)
        sa1[:, :, cols] = total.astype(BF16)

    pl.loop(0, HALF // CHUNK)(sum_a)
    da_2 = net.ring("z", lambda d: sa1.at[net.coord("z", d)], lambda d: da2.at[d - 1])
    arrive(db_1)

    def sum_b(i):
        cols = pl.ds(pl.multiple_of(i * CHUNK, CHUNK), CHUNK)
        far = pl.ds(pl.multiple_of(HALF + i * CHUNK, CHUNK), CHUNK)
        total = pd[z, :, :, far].astype(F32)
        for d in range(3):
            total += db1[d, :, :, cols].astype(F32)
        sb1[:, :, cols] = total.astype(BF16)

    pl.loop(0, HALF // CHUNK)(sum_b)
    db_2 = net.ring("y", lambda d: sb1.at[net.coord("y", d)], lambda d: db2.at[d - 1])

    arrive(dk_4)
    arrive(dv_4)
    feats = feat_all[...].reshape(512, 256)
    d_feats = jnp.zeros((512, 256), F32)
    for h in range(8):
        for at, full in ((h * HD, dkg), (1024 + h * HD, dvg)):
            grad = full[h // 2, h % 2].reshape(512, HD)
            gkv_out[:, at : at + HD] = dot(feats, grad, TN).astype(BF16)
            d_feats += dot(grad, wkv[:, at : at + HD], NT)
    df[...] = d_feats.reshape(4, 128, 256)
    f_1 = net.ring("s", lambda d: df.at[net.coord("s", d)], lambda d: dfr.at[d - 1])

    arrive(da_2)
    arrive(db_2)

    def sum_ab(i):
        cols = pl.ds(pl.multiple_of(i * CHUNK, CHUNK), CHUNK)
        ta = sa1[z, :, cols].astype(F32)
        tb = sb1[y, :, cols].astype(F32)
        for d in range(3):
            ta += da2[d, :, cols].astype(F32)
            tb += db2[d, :, cols].astype(F32)
        own_d[:8, cols] = jnp.where(x == 0, ta[:8], ta[8:])
        own_d[8:, cols] = jnp.where(x == 0, tb[:8], tb[8:])
        fold_d[:, cols] = jnp.concatenate(
            [jnp.where(x == 0, ta[8:], ta[:8]), jnp.where(x == 0, tb[8:], tb[:8])], axis=0
        ).astype(BF16)

    pl.loop(0, HALF // CHUNK)(sum_ab)
    d_x = net.send("x", 1, fold_d, from_d)

    arrive(f_1)
    img = df[s]
    for d in range(3):
        img += dfr[d]
    img_s[...] = img.reshape(4, 32, 256)
    img_z[z] = img_s[z]
    f_2 = net.ring("z", lambda d: img_s.at[net.coord("z", d)], lambda d: img_z.at[z])

    g_3.wait_recv()
    gg_out[...] = gx2[0] + gx2[1]
    d_x.wait_recv()
    both = own_d[...] + from_d[...].astype(F32)
    dn = jnp.concatenate([both[:8], both[8:]], axis=1)
    xf = tok_ref[...].astype(F32)
    scaled = dn * gain_ref[...]
    gx_out[...] = (
        rinv * scaled - xf * rinv * rinv * rinv * jnp.mean(xf * scaled, axis=-1, keepdims=True)
    ).astype(BF16)
    arrive(f_2)
    img_x[x] = img_z[:, pl.ds(pl.multiple_of(x * 16, 16), 16), :]
    far = pl.ds(pl.multiple_of((1 - x) * 16, 16), 16)
    f_3 = net.send("x", 1, img_z.at[:, far], img_x.at[x])
    f_3.wait_recv()

    def tile(d):
        return pl.ds(pl.multiple_of((net.coord("y", d) // 2) * 8, 8), 8)

    gi_all[y] = img_x[:, :, tile(0), :]
    f_4 = net.ring("y", lambda d: img_x.at[:, :, tile(d)], lambda d: gi_all.at[y])
    arrive(f_4)
    for m in range(32):
        tile_m = gi_all[m % 4, (m // 4) % 2, m // 8]
        gi_out[:, m * VCOLS : (m + 1) * VCOLS] = jnp.where(y % 2 == 0, tile_m[:4], tile_m[4:])[:, :VCOLS]
    for copy in stores:
        copy.wait()
    net.finish()


def run_layer(tokens, cotangent, gain_row, visible, units, w_q, w_o, w_kv):
    any_spec = pl.BlockSpec(memory_space=pl.ANY)
    vmem = pl.BlockSpec(memory_space=pltpu.VMEM)
    smem = pl.BlockSpec(memory_space=pltpu.SMEM)
    shape = jax.ShapeDtypeStruct
    b, f = (lambda *dims: pltpu.VMEM(dims, BF16)), (lambda *dims: pltpu.VMEM(dims, F32))
    return pl.pallas_call(
        layer_kernel,
        out_shape=(
            shape((4, 4, 16, D), BF16),
            shape((4, 4, 16, D), BF16),
            shape((TOK, 256), BF16),
            shape((TOK, 256), BF16),
            shape((256, 2048), BF16),
            shape((8, D), BF16),
            shape((8, 1024), F32),
            shape((4, 32 * VCOLS), F32),
        ),
        in_specs=[vmem, vmem, vmem, smem, vmem, any_spec, any_spec, any_spec],
        out_specs=(any_spec, any_spec, vmem, vmem, vmem, vmem, vmem, vmem),
        scratch_shapes=[
            b(4, 4, 16, D), b(4, 4, 16, D), b(D, 256), b(256, D), b(256, 2048),
            f(4, 4, 2, 8, HD), f(4, 4, 2, 8, HD), f(2, 4, 4, 8, HD), b(4, 128, 256),
            b(16, HALF), b(16, HALF), b(16, HALF), b(16, HALF),
            b(4, 2, 4, 128, HD), b(4, 2, 4, 128, HD),
            b(3, 4, 2, 128, HD), b(3, 2, 4, 128, HD),
            f(4, 2, 128, HD), f(2, 4, 128, HD),
            f(3, 2, 128, HD), f(3, 2, 128, HD),
            f(2, 128, HD), f(2, 128, HD),
            f(128, HD), f(128, HD),
            b(4, 128, HD), b(4, 128, HD),
            b(4, 128, HD), b(4, 128, HD), b(3, 128, HD), b(3, 128, HD),
            b(4, 2, 4, 128, HD), b(4, 2, 4, 128, HD),
            b(4, 4, 16, D),
            b(3, 4, 16, HALF), b(3, 4, 16, HALF),
            b(4, 16, HALF), b(4, 16, HALF),
            b(3, 16, HALF), b(3, 16, HALF),
            f(16, HALF), b(16, HALF), b(16, HALF),
            f(4, 128, 256), f(3, 128, 256),
            f(4, 32, 256), f(4, 32, 256), f(2, 4, 16, 256), f(4, 2, 4, 8, 256),
            f(1, D), f(4, 8, 1024), f(4, 8, 1024), f(2, 8, 1024),
            pltpu.SemaphoreType.DMA((NSEM,)),
            pltpu.SemaphoreType.DMA((NSEM,)),
            pltpu.SemaphoreType.DMA((5,)),
        ],
        compiler_params=pltpu.CompilerParams(
            collective_id=0, has_side_effects=True, vmem_limit_bytes=58 * 1024 * 1024
        ),
        cost_estimate=pl.CostEstimate(
            flops=6 * 10**9, bytes_accessed=20 * 2**20, transcendentals=2 * 256 * 512
        ),
        name="layer",
    )(tokens, cotangent, gain_row, visible, units, w_q, w_o, w_kv)


def weight_kernel(n_ref, c_ref, attn_ref, dq_ref, gkv_ref, gq_ref, go_ref, gk_ref):
    width = n_ref.shape[-1]
    gq_ref[...] = dot(n_ref[...].reshape(TOK, width), dq_ref[...], TN).astype(BF16)
    go_ref[...] = dot(attn_ref[...], c_ref[...].reshape(TOK, width), TN).astype(BF16)
    gk_ref[...] = gkv_ref[:VCOLS, :]


def weight_grads(normed, cotangent, attn, d_query, grad_kv):
    steps = 8
    width, kv_width = D // steps, 2048 // steps
    shape = jax.ShapeDtypeStruct
    wide = pl.BlockSpec((4, 4, 16, width), lambda i: (0, 0, 0, i))
    whole = pl.BlockSpec((TOK, 256), lambda i: (0, 0))
    return pl.pallas_call(
        weight_kernel,
        grid=(steps,),
        out_shape=(
            shape((D, 256), BF16),
            shape((256, D), BF16),
            shape((VCOLS, 2048), BF16),
        ),
        in_specs=[wide, wide, whole, whole, pl.BlockSpec((256, kv_width), lambda i: (0, i))],
        out_specs=(
            pl.BlockSpec((width, 256), lambda i: (i, 0)),
            pl.BlockSpec((256, width), lambda i: (0, i)),
            pl.BlockSpec((VCOLS, kv_width), lambda i: (0, i)),
        ),
        compiler_params=pltpu.CompilerParams(vmem_limit_bytes=32 * 1024 * 1024),
        name="weight_grads",
    )(normed, cotangent, attn, d_query, grad_kv)


def per_device(tokens, upstream, norm_gain, w_query, w_output, w_keyvalue, image_feats, visible):
    units = image_feats.astype(F32).reshape(4, 32, VCOLS)
    units = jnp.pad(units, ((0, 0), (0, 0), (0, 256 - VCOLS))).reshape(4, 32, 2, HD)
    units = units.transpose(1, 2, 0, 3).reshape(4, 2, 4, 8, HD)
    normed, cotangent, attn, d_query, grad_kv, grad_x, grad_g, grad_image = run_layer(
        tokens[0], upstream[0], norm_gain, visible, units, w_query[0], w_output[0], w_keyvalue[0]
    )
    grad_q, grad_out, grad_kv = weight_grads(normed, cotangent, attn, d_query, grad_kv)
    return (
        grad_x[None],
        grad_g.reshape(1, D),
        grad_q[None],
        grad_out[None],
        grad_kv[None],
        grad_image,
    )


def solution(mesh):
    placed = (
        P("section", "mp", None),
        P("section", "mp", None),
        P("section", None),
        P("section", None, "mp"),
        P("section", "mp", None),
        P("section", "mp", None),
        P(("section", "mp"), None),
        P(),
    )
    return jax.shard_map(
        per_device,
        mesh=mesh,
        in_specs=placed,
        out_specs=(
            P("section", "mp", None),
            P("section", None),
            P("section", None, "mp"),
            P("section", "mp", None),
            P("section", "mp", None),
            P(("section", "mp"), None),
        ),
        check_vma=False,
    )
```

```python
import jax
import jax.numpy as jnp
from jax import lax
from jax.experimental import pallas as pl
from jax.experimental.pallas import tpu as pltpu
from jax.sharding import PartitionSpec as P

MESH = pl.DeviceIdType.MESH
F32 = jnp.float32
BF16 = jnp.bfloat16
TOK = 256
D = 8192
HALF = D // 2
QUART = D // 4
CHUNK = 1024
HD = 128
VCOLS = 240
SCALE = HD ** (-0.5)
NSEM = 192

NT = (((1,), (1,)), ((), ()))
TN = (((0,), (0,)), ((), ()))


def dot(a, b, dims=(((1,), (0,)), ((), ()))):
    return lax.dot_general(a, b, dims, preferred_element_type=F32)


class Links:
    def __init__(self, send_sems, recv_sems):
        self.s = lax.axis_index("section")
        index = lax.axis_index("mp")
        self.z, self.x, self.y = index // 8, (index // 4) % 2, index % 4
        self.send_sems, self.recv_sems = send_sems, recv_sems
        self.copies = []

    def coord(self, axis, d):
        if axis == "x":
            return (self.x + d) % 2
        return (getattr(self, axis) + d) % 4

    def peer(self, axis, d):
        at = {"s": self.s, "z": self.z, "x": self.x, "y": self.y}
        at[axis] = self.coord(axis, d)
        return (at["s"], at["z"] * 8 + at["x"] * 4 + at["y"])

    def barrier(self):
        sem = pltpu.get_barrier_semaphore()
        peers = [(a, d) for a in ("z", "y", "s") for d in (1, 2, 3)] + [("x", 1)]
        for a, d in peers:
            pl.semaphore_signal(sem, inc=1, device_id=self.peer(a, d), device_id_type=MESH)
        pl.semaphore_wait(sem, len(peers))

    def send(self, axis, d, src, dst):
        at = len(self.copies)
        copy = pltpu.make_async_remote_copy(
            src_ref=src,
            dst_ref=dst,
            send_sem=self.send_sems.at[at],
            recv_sem=self.recv_sems.at[at],
            device_id=self.peer(axis, d),
            device_id_type=MESH,
        )
        copy.start()
        self.copies.append(copy)
        return copy

    def ring(self, axis, src, dst):
        return [self.send(axis, d, src(d), dst(d)) for d in (1, 3, 2)]

    def finish(self):
        for copy in self.copies:
            copy.wait_send()


def arrive(copies):
    for copy in copies:
        copy.wait_recv()


class Gather:
    def __init__(self, net, full, first, second, start):
        self.net, self.full, self.first, self.second = net, full, first, second
        self.cols = pl.ds(start, HALF)
        self.sub = (pl.ds(start, QUART), pl.ds(start + QUART, QUART))

    def block(self, i, j, cols):
        i, j = self.net.coord(self.first, i), self.net.coord(self.second, j)
        return self.full.at[i, j, :, cols] if self.first == "z" else self.full.at[j, i, :, cols]

    def push(self, axis, d, i, j, cols):
        block = self.block(i, j, cols)
        return self.net.send(axis, d, block, block)

    def start(self):
        self.near = [self.push(self.first, d, 0, 0, self.cols) for d in (1, 3)]
        self.lines = [[self.push(self.second, d, 0, 0, self.cols) for d in (1, 3)]]

    def middle(self):
        self.far = []
        for copy, d, sub in zip(self.near, (1, 3), self.sub):
            copy.wait_recv()
            self.far.append(self.push(self.first, d, 4 - d, 0, sub))
            self.lines.append([self.push(self.second, e, 4 - d, 0, self.cols) for e in (1, 3)])

    def spread(self):
        arrive(self.far)
        self.lines.append([self.push(self.second, e, 2, 0, self.cols) for e in (1, 3)])

    def forward(self):
        self.last = []
        for i, line in zip((0, 3, 1, 2), self.lines):
            for copy, d, sub in zip(line, (1, 3), self.sub):
                copy.wait_recv()
                self.last.append(self.push(self.second, d, i, 4 - d, sub))

    def end(self):
        arrive(self.last)


def columns(start, stop, body, step=CHUNK):
    @pl.loop(0, (stop - start) // step)
    def _(i):
        body(pl.ds(pl.multiple_of(start + i * step, step), step))


def layer_kernel(
    tok_ref, cot_ref, gain_ref, vis_ref, unit_ref, wq_hbm, wo_hbm, wkv_hbm,
    n_out, c_out, attn_out, dq_out, gkv_out, gx_out, gg_out, gi_out,
    n_all, c_all, wq, wo, wkv,
    u_y, u_z, u_x, feat_all,
    fold_n, fold_c, from_n, from_c,
    feat_t, pk, pv, k_y, k_z, v_y, v_z, kv_1, kv_2, kv_3, kv_4, keys, values,
    dk, dv, rk, rv, dkg, dvg,
    pd, via_a, via_b, relay_a, relay_b, near_a, near_b, sa1, sb1, da2, db2, own_d, fold_d, from_d,
    df, dfr, img_s, img_z, img_x, gi_all, gain_part, gz, gy, gx2,
    send_sems, recv_sems, local_sems,
):
    net = Links(send_sems, recv_sems)
    s, z, x, y = net.s, net.z, net.x, net.y
    loads = []
    wkv[VCOLS:, :] = jnp.zeros((256 - VCOLS, 2048), BF16)
    for i, (src, dst) in enumerate(((wkv_hbm, wkv.at[:VCOLS]), (wq_hbm, wq), (wo_hbm, wo))):
        copy = pltpu.make_async_copy(src, dst, local_sems.at[i])
        copy.start()
        loads.append(copy)
    net.barrier()

    u_y[y] = unit_ref[:, :, y]
    u_1 = net.ring("y", lambda d: unit_ref.at[:, :, net.coord("y", d)], lambda d: u_y.at[y])

    xf = tok_ref[...].astype(F32)
    rinv = lax.rsqrt(jnp.mean(xf * xf, axis=-1, keepdims=True) + 1e-05)

    def normed_at(cols):
        return tok_ref[:, cols].astype(F32) * rinv * gain_ref[:, cols]

    def fold_step(at, into):
        def step(i):
            lo = pl.ds(pl.multiple_of(i * CHUNK, CHUNK), CHUNK)
            hi = pl.ds(pl.multiple_of(HALF + i * CHUNK, CHUNK), CHUNK)
            into[:, lo] = jnp.concatenate([at(lo), at(hi)], axis=0).astype(BF16)

        pl.loop(0, HALF // CHUNK)(step)

    fold_step(normed_at, fold_n)
    x_n = net.send("x", 1, fold_n, from_n)
    fold_step(lambda cols: cot_ref[:, cols].astype(F32), fold_c)
    x_c = net.send("x", 1, fold_c, from_c)
    arrive(u_1)
    u_z[z] = u_y[:, z]
    u_2 = net.ring("z", lambda d: u_y.at[:, net.coord("z", d)], lambda d: u_z.at[z])

    def unfold(folded, received, full):
        def step(i):
            lo = pl.ds(pl.multiple_of(i * CHUNK, CHUNK), CHUNK)
            hi = pl.ds(pl.multiple_of(HALF + i * CHUNK, CHUNK), CHUNK)
            mine = folded[:, lo].astype(F32)
            other = received[:, lo].astype(F32)
            for at, cols in ((0, lo), (8, hi)):
                a, b = mine[at : at + 8], other[at : at + 8]
                first = jnp.where(x == 0, a, b)
                second = jnp.where(x == 0, b, a)
                full[z, y, :, cols] = jnp.concatenate([first, second], axis=0).astype(BF16)

        pl.loop(0, HALF // CHUNK)(step)

    a_cols, b_cols = pl.ds(0, HALF), pl.ds(HALF, HALF)
    gather_n = [Gather(net, n_all, "z", "y", 0), Gather(net, n_all, "y", "z", HALF)]
    gather_c = [Gather(net, c_all, "z", "y", 0), Gather(net, c_all, "y", "z", HALF)]
    x_n.wait_recv()
    unfold(fold_n, from_n, n_all)
    for half in gather_n:
        half.start()

    arrive(u_2)
    u_x[x] = u_z[:, :, x]
    u_3 = net.send("x", 1, u_z.at[:, :, 1 - x], u_x.at[x])
    x_c.wait_recv()
    unfold(fold_c, from_c, c_all)
    for half in gather_n:
        half.middle()

    u_3.wait_recv()
    units = u_x[...].reshape(256, HD).astype(BF16)
    row = lax.broadcasted_iota(jnp.int32, (128, 256), 0)
    col = lax.broadcasted_iota(jnp.int32, (128, 256), 1)
    at = (((row // 16) % 2 * 4 + row // 32) * 4 + (row // 4) % 4) * 8 + row % 4
    for half in range(2):
        pick = jnp.where(col == at + 4 * half, 1.0, 0.0).astype(BF16)
        feat_all[s, :, half * HD : (half + 1) * HD] = dot(pick, units).astype(BF16)
    f_0 = net.ring("s", lambda d: feat_all.at[s], lambda d: feat_all.at[s])
    for half in gather_n:
        half.spread()
    arrive(f_0)

    loads[0].wait()

    def kv_step(h):
        cols = pl.ds(pl.multiple_of(h * HD, HD), HD)
        vcols = pl.ds(pl.multiple_of(1024 + h * HD, HD), HD)
        feats = feat_all[...].reshape(512, 256)
        pk[h // 2, h % 2] = dot(feats, wkv[:, cols]).reshape(4, 128, HD)
        pv[h // 2, h % 2] = dot(feats, wkv[:, vcols]).astype(BF16).reshape(4, 128, HD)

    pl.loop(0, 8)(kv_step)

    def term(part, axis, at, rows):
        return part.at[:, :, at, rows] if axis == "y" else part.at[at, :, :, rows]

    chains = []
    for part, y_buf, z_buf in ((pk, k_y, k_z), (pv, v_y, v_z)):
        for n, (axis, buf) in enumerate((("y", y_buf), ("z", z_buf))):
            rows = pl.ds(64 * n, 64)
            copies = net.ring(
                axis,
                lambda d: term(part, axis, net.coord(axis, d), rows),
                lambda d: buf.at[d - 1],
            )
            chains.append([part, axis, n, rows, buf, copies])
    for half in gather_n:
        half.forward()
    for half in gather_c:
        half.start()
    for c, (part, axis, n, rows, buf, copies) in enumerate(chains):
        arrive(copies)
        for a in range(4):
            for b in range(2):
                at = (a, b) if axis == "y" else (b, a)
                own = part[a, b, y, rows] if axis == "y" else part[z, b, a, rows]
                total = own.astype(F32)
                for d in range(3):
                    total += buf[(d, *at)].astype(F32)
                kv_1[(c, a, b)] = total
        chains[c][5] = net.ring(
            "z" if axis == "y" else "y",
            lambda d: kv_1.at[c, net.coord("z" if axis == "y" else "y", d)],
            lambda d: kv_2.at[c, d - 1],
        )
    for half in gather_c:
        half.middle()
    kv_x = []
    for c, (part, axis, n, rows, buf, copies) in enumerate(chains):
        arrive(copies)
        mine = z if axis == "y" else y
        for b in range(2):
            total = kv_1[c, mine, b]
            for d in range(3):
                total += kv_2[c, d, b]
            kv_3[c, b] = total
        kv_x.append(net.send("x", 1, kv_3.at[c, 1 - x], kv_4.at[c]))
    for half in gather_c:
        half.spread()
    for c, (part, axis, n, rows, buf, copies) in enumerate(chains):
        kv_x[c].wait_recv()
        (keys if c < 2 else values)[y, 64 * n : 64 * n + 64] = (kv_3[c, x] + kv_4[c]).astype(BF16)
    k_3 = net.ring("y", lambda d: keys.at[y], lambda d: keys.at[y])
    v_3 = net.ring("y", lambda d: values.at[y], lambda d: values.at[y])
    feat_t[...] = feat_all[...].reshape(512, 256).astype(F32).T.astype(BF16)

    for half in gather_n:
        half.end()
    stores = []
    copy = pltpu.make_async_copy(n_all, n_out, local_sems.at[3])
    copy.start()
    stores.append(copy)
    loads[1].wait()

    def query_step(i, acc):
        cols = pl.ds(pl.multiple_of(i * CHUNK, CHUNK), CHUNK)
        return acc + dot(n_all[:, :, :, cols].reshape(TOK, CHUNK), wq[cols, :])

    query = lax.fori_loop(0, D // CHUNK, query_step, jnp.zeros((TOK, 256), F32)).astype(BF16)

    for half in gather_c:
        half.forward()
    arrive(k_3)
    arrive(v_3)
    key = keys[...].reshape(512, HD)
    value = values[...].reshape(512, HD)
    image_of = lax.broadcasted_iota(jnp.int32, (TOK, 512), 1) // 128
    late = lax.broadcasted_iota(jnp.int32, (TOK, 512), 0) >= 128
    allowed = image_of < jnp.where(late, vis_ref[1], vis_ref[0])
    probs, weights = [], []
    for j in range(2):
        q = query[:, j * HD : (j + 1) * HD]
        scores = jnp.where(allowed, dot(q, key, NT) * SCALE, -1e30)
        expo = jnp.exp(scores - jnp.max(scores, axis=-1, keepdims=True))
        prob = expo / jnp.sum(expo, axis=-1, keepdims=True)
        probs.append(prob)
        weights.append(prob.astype(BF16))
        attn_out[:, j * HD : (j + 1) * HD] = dot(weights[j], value).astype(BF16)

    for half in gather_c:
        half.end()
    copy = pltpu.make_async_copy(c_all, c_out, local_sems.at[4])
    copy.start()
    stores.append(copy)
    loads[2].wait()

    def d_attn_step(i, acc):
        cols = pl.ds(pl.multiple_of(i * CHUNK, CHUNK), CHUNK)
        return acc + dot(c_all[:, :, :, cols].reshape(TOK, CHUNK), wo[:, cols], NT)

    d_attn = lax.fori_loop(0, D // CHUNK, d_attn_step, jnp.zeros((TOK, 256), F32)).astype(BF16)
    d_key = jnp.zeros((512, HD), F32)
    d_value = jnp.zeros((512, HD), F32)
    for j in range(2):
        heads = slice(j * HD, (j + 1) * HD)
        da = d_attn[:, heads]
        d_prob = dot(da, value, NT)
        delta = jnp.sum(probs[j] * d_prob, axis=-1, keepdims=True)
        d_score = (probs[j] * (d_prob - delta) * SCALE).astype(BF16)
        dq_out[:, heads] = dot(d_score, key).astype(BF16)
        d_key += dot(d_score, query[:, heads], TN)
        d_value += dot(weights[j], da, TN)
    dk[...] = d_key.astype(BF16).reshape(4, 128, HD)
    dv[...] = d_value.astype(BF16).reshape(4, 128, HD)
    dk_1 = net.ring("y", lambda d: dk.at[net.coord("y", d)], lambda d: rk.at[d - 1])
    dv_1 = net.ring("y", lambda d: dv.at[net.coord("y", d)], lambda d: rv.at[d - 1])

    def d_normed_step(cols):
        part = dot(dq_out[...], wq[cols, :], NT)
        pd[:, :, :, cols] = part.astype(BF16).reshape(4, 4, 16, CHUNK)
        normed = n_all[:, :, :, cols].reshape(TOK, CHUNK).astype(F32)
        gain_part[:, cols] = jnp.sum(part * normed, axis=0, keepdims=True) / gain_ref[:, cols]

    def line(axis, d, cols):
        at = net.coord(axis, d)
        return pd.at[:, at, :, cols] if axis == "y" else pd.at[at, :, :, cols]

    def reduce_start(axis, start, via, near):
        subs = (pl.ds(start, QUART), pl.ds(start + QUART, QUART))
        far = [
            net.send(axis, d, line(axis, 2, subs[n]), via.at[n]) for n, d in enumerate((1, 3))
        ]
        direct = [
            net.send(axis, d, line(axis, d, subs[1 - n]), near.at[n, :, :, pl.ds((1 - n) * QUART, QUART)])
            for n, d in enumerate((1, 3))
        ]
        return far, direct

    def reduce_on(axis, start, via, relay, near, far):
        out = []
        for n, d in enumerate((1, 3)):
            far[n].wait_recv()
            at = net.coord(axis, d)

            def step(i):
                cols = pl.ds(pl.multiple_of(i * CHUNK, CHUNK), CHUNK)
                own = pl.ds(pl.multiple_of(start + n * QUART + i * CHUNK, CHUNK), CHUNK)
                mine = pd[:, at, :, own] if axis == "y" else pd[at, :, :, own]
                relay[n, :, :, cols] = (mine.astype(F32) + via[n, :, :, cols].astype(F32)).astype(BF16)

            pl.loop(0, QUART // CHUNK)(step)
            out.append(net.send(axis, d, relay.at[n], near.at[n, :, :, pl.ds(n * QUART, QUART)]))
        return out

    def reduce_end(axis, start, near, copies, into):
        arrive(copies)

        def step(i):
            cols = pl.ds(pl.multiple_of(i * CHUNK, CHUNK), CHUNK)
            own = pl.ds(pl.multiple_of(start + i * CHUNK, CHUNK), CHUNK)
            total = (pd[:, y, :, own] if axis == "y" else pd[z, :, :, own]).astype(F32)
            into[:, :, cols] = (
                total + near[0, :, :, cols].astype(F32) + near[1, :, :, cols].astype(F32)
            ).astype(BF16)

        pl.loop(0, HALF // CHUNK)(step)

    columns(0, HALF, d_normed_step)
    da_far, da_near = reduce_start("y", 0, via_a, near_a)
    columns(HALF, D, d_normed_step)
    db_far, db_near = reduce_start("z", HALF, via_b, near_b)
    for i in range(8):
        gz[z, i : i + 1, :] = gain_part[:, i * 1024 : (i + 1) * 1024]
    g_1 = net.ring("z", lambda d: gz.at[z], lambda d: gz.at[z])

    arrive(dk_1)
    arrive(dv_1)
    total = dk[y].astype(F32)
    vtotal = dv[y].astype(F32)
    for d in range(3):
        total += rk[d].astype(F32)
        vtotal += rv[d].astype(F32)
    dkg[z, x, y] = total.astype(BF16)
    dvg[z, x, y] = vtotal.astype(BF16)
    mine_k, mine_v = dkg.at[z, x, y], dvg.at[z, x, y]
    dk_2 = net.send("x", 1, mine_k, mine_k)
    dv_2 = net.send("x", 1, mine_v, mine_v)
    dk_2.wait_recv()
    dv_2.wait_recv()
    pair_k, pair_v = dkg.at[z, :, y], dvg.at[z, :, y]
    dk_3 = net.ring("z", lambda d: pair_k, lambda d: pair_k)
    dv_3 = net.ring("y", lambda d: pair_v, lambda d: pair_v)
    da_near += reduce_on("y", 0, via_a, relay_a, near_a, da_far)
    arrive(dk_3)
    line_k = dkg.at[:, :, y]
    dk_4 = net.ring("y", lambda d: line_k, lambda d: line_k)
    arrive(dv_3)
    line_v = dvg.at[z]
    dv_4 = net.ring("z", lambda d: line_v, lambda d: line_v)
    db_near += reduce_on("z", HALF, via_b, relay_b, near_b, db_far)
    arrive(g_1)
    gy[y] = (gz[0] + gz[1]) + (gz[2] + gz[3])
    g_2 = net.ring("y", lambda d: gy.at[y], lambda d: gy.at[y])

    reduce_end("y", 0, near_a, da_near, sa1)
    da_2 = net.ring("z", lambda d: sa1.at[net.coord("z", d)], lambda d: da2.at[d - 1])
    reduce_end("z", HALF, near_b, db_near, sb1)
    db_2 = net.ring("y", lambda d: sb1.at[net.coord("y", d)], lambda d: db2.at[d - 1])
    arrive(g_2)
    gx2[x] = (gy[0] + gy[1]) + (gy[2] + gy[3])
    g_3 = net.send("x", 1, gx2.at[x], gx2.at[x])

    arrive(dk_4)
    arrive(dv_4)
    d_feats = jnp.zeros((512, 256), F32)
    for h in range(8):
        both = jnp.concatenate(
            [full[h // 2, h % 2].reshape(512, HD) for full in (dkg, dvg)], axis=1
        )
        weights_h = jnp.concatenate(
            [wkv[:, at : at + HD] for at in (h * HD, 1024 + h * HD)], axis=1
        )
        d_feats += dot(both, weights_h, NT)
    df[...] = d_feats.astype(BF16).reshape(4, 128, 256)
    f_1 = net.ring("s", lambda d: df.at[net.coord("s", d)], lambda d: dfr.at[d - 1])
    for h in range(8):
        for at, full in ((h * HD, dkg), (1024 + h * HD, dvg)):
            gkv_out[:, at : at + HD] = dot(feat_t[...], full[h // 2, h % 2].reshape(512, HD)).astype(BF16)

    arrive(da_2)
    arrive(db_2)

    def sum_ab(i):
        cols = pl.ds(pl.multiple_of(i * CHUNK, CHUNK), CHUNK)
        ta = sa1[z, :, cols].astype(F32)
        tb = sb1[y, :, cols].astype(F32)
        for d in range(3):
            ta += da2[d, :, cols].astype(F32)
            tb += db2[d, :, cols].astype(F32)
        own_d[:8, cols] = jnp.where(x == 0, ta[:8], ta[8:])
        own_d[8:, cols] = jnp.where(x == 0, tb[:8], tb[8:])
        fold_d[:, cols] = jnp.concatenate(
            [jnp.where(x == 0, ta[8:], ta[:8]), jnp.where(x == 0, tb[8:], tb[:8])], axis=0
        ).astype(BF16)

    pl.loop(0, HALF // CHUNK)(sum_ab)
    d_x = net.send("x", 1, fold_d, from_d)

    arrive(f_1)
    img = df[s].astype(F32)
    for d in range(3):
        img += dfr[d].astype(F32)
    img_s[...] = img.reshape(4, 32, 256)
    img_z[z] = img_s[z]
    f_2 = net.ring("z", lambda d: img_s.at[net.coord("z", d)], lambda d: img_z.at[z])

    g_3.wait_recv()
    gg_out[...] = gx2[0] + gx2[1]
    d_x.wait_recv()
    both = own_d[...] + from_d[...].astype(F32)
    dn = jnp.concatenate([both[:8], both[8:]], axis=1)
    xf = tok_ref[...].astype(F32)
    scaled = dn * gain_ref[...]
    gx_out[...] = (
        rinv * scaled - xf * rinv * rinv * rinv * jnp.mean(xf * scaled, axis=-1, keepdims=True)
    ).astype(BF16)
    arrive(f_2)
    img_x[x] = img_z[:, pl.ds(pl.multiple_of(x * 16, 16), 16), :]
    far = pl.ds(pl.multiple_of((1 - x) * 16, 16), 16)
    f_3 = net.send("x", 1, img_z.at[:, far], img_x.at[x])
    f_3.wait_recv()

    def tile(d):
        return pl.ds(pl.multiple_of((net.coord("y", d) // 2) * 8, 8), 8)

    gi_all[y] = img_x[:, :, tile(0), :]
    f_4 = net.ring("y", lambda d: img_x.at[:, :, tile(d)], lambda d: gi_all.at[y])
    arrive(f_4)
    for m in range(32):
        tile_m = gi_all[m % 4, (m // 4) % 2, m // 8]
        gi_out[:, m * VCOLS : (m + 1) * VCOLS] = jnp.where(y % 2 == 0, tile_m[:4], tile_m[4:])[:, :VCOLS]
    for copy in stores:
        copy.wait()
    net.finish()


def run_layer(tokens, cotangent, gain_row, visible, units, w_q, w_o, w_kv):
    any_spec = pl.BlockSpec(memory_space=pl.ANY)
    vmem = pl.BlockSpec(memory_space=pltpu.VMEM)
    smem = pl.BlockSpec(memory_space=pltpu.SMEM)
    shape = jax.ShapeDtypeStruct
    b, f = (lambda *dims: pltpu.VMEM(dims, BF16)), (lambda *dims: pltpu.VMEM(dims, F32))
    return pl.pallas_call(
        layer_kernel,
        out_shape=(
            shape((4, 4, 16, D), BF16),
            shape((4, 4, 16, D), BF16),
            shape((TOK, 256), BF16),
            shape((TOK, 256), BF16),
            shape((256, 2048), BF16),
            shape((8, D), BF16),
            shape((8, 1024), F32),
            shape((4, 32 * VCOLS), F32),
        ),
        in_specs=[vmem, vmem, vmem, smem, vmem, any_spec, any_spec, any_spec],
        out_specs=(any_spec, any_spec, vmem, vmem, vmem, vmem, vmem, vmem),
        scratch_shapes=[
            b(4, 4, 16, D), b(4, 4, 16, D), b(D, 256), b(256, D), b(256, 2048),
            f(4, 4, 2, 8, HD), f(4, 4, 2, 8, HD), f(2, 4, 4, 8, HD), b(4, 128, 256),
            b(16, HALF), b(16, HALF), b(16, HALF), b(16, HALF),
            b(256, 512), f(4, 2, 4, 128, HD), b(4, 2, 4, 128, HD),
            f(3, 4, 2, 64, HD), f(3, 2, 4, 64, HD), b(3, 4, 2, 64, HD), b(3, 2, 4, 64, HD),
            f(4, 4, 2, 64, HD), f(4, 3, 2, 64, HD), f(4, 2, 64, HD), f(4, 64, HD),
            b(4, 128, HD), b(4, 128, HD),
            b(4, 128, HD), b(4, 128, HD), b(3, 128, HD), b(3, 128, HD),
            b(4, 2, 4, 128, HD), b(4, 2, 4, 128, HD),
            b(4, 4, 16, D),
            b(2, 4, 16, QUART), b(2, 4, 16, QUART), b(2, 4, 16, QUART), b(2, 4, 16, QUART),
            b(2, 4, 16, HALF), b(2, 4, 16, HALF),
            b(4, 16, HALF), b(4, 16, HALF),
            b(3, 16, HALF), b(3, 16, HALF),
            f(16, HALF), b(16, HALF), b(16, HALF),
            b(4, 128, 256), b(3, 128, 256),
            f(4, 32, 256), f(4, 32, 256), f(2, 4, 16, 256), f(4, 2, 4, 8, 256),
            f(1, D), f(4, 8, 1024), f(4, 8, 1024), f(2, 8, 1024),
            pltpu.SemaphoreType.DMA((NSEM,)),
            pltpu.SemaphoreType.DMA((NSEM,)),
            pltpu.SemaphoreType.DMA((5,)),
        ],
        compiler_params=pltpu.CompilerParams(
            collective_id=0, has_side_effects=True, vmem_limit_bytes=58 * 1024 * 1024
        ),
        cost_estimate=pl.CostEstimate(
            flops=6 * 10**9, bytes_accessed=20 * 2**20, transcendentals=2 * 256 * 512
        ),
        name="layer",
    )(tokens, cotangent, gain_row, visible, units, w_q, w_o, w_kv)


def weight_kernel(n_ref, c_ref, attn_ref, dq_ref, gkv_ref, gq_ref, go_ref, gk_ref):
    width = n_ref.shape[-1]
    gq_ref[...] = dot(n_ref[...].reshape(TOK, width), dq_ref[...], TN).astype(BF16)
    go_ref[...] = dot(attn_ref[...], c_ref[...].reshape(TOK, width), TN).astype(BF16)
    gk_ref[...] = gkv_ref[:VCOLS, :]


def weight_grads(normed, cotangent, attn, d_query, grad_kv):
    steps = 8
    width, kv_width = D // steps, 2048 // steps
    shape = jax.ShapeDtypeStruct
    wide = pl.BlockSpec((4, 4, 16, width), lambda i: (0, 0, 0, i))
    whole = pl.BlockSpec((TOK, 256), lambda i: (0, 0))
    return pl.pallas_call(
        weight_kernel,
        grid=(steps,),
        out_shape=(
            shape((D, 256), BF16),
            shape((256, D), BF16),
            shape((VCOLS, 2048), BF16),
        ),
        in_specs=[wide, wide, whole, whole, pl.BlockSpec((256, kv_width), lambda i: (0, i))],
        out_specs=(
            pl.BlockSpec((width, 256), lambda i: (i, 0)),
            pl.BlockSpec((256, width), lambda i: (0, i)),
            pl.BlockSpec((VCOLS, kv_width), lambda i: (0, i)),
        ),
        compiler_params=pltpu.CompilerParams(vmem_limit_bytes=62 * 1024 * 1024),
        name="weight_grads",
    )(normed, cotangent, attn, d_query, grad_kv)


def per_device(tokens, upstream, norm_gain, w_query, w_output, w_keyvalue, image_feats, visible):
    units = image_feats.astype(F32).reshape(4, 32, VCOLS)
    units = jnp.pad(units, ((0, 0), (0, 0), (0, 256 - VCOLS))).reshape(4, 32, 2, HD)
    units = units.transpose(1, 2, 0, 3).reshape(4, 2, 4, 8, HD)
    normed, cotangent, attn, d_query, grad_kv, grad_x, grad_g, grad_image = run_layer(
        tokens[0], upstream[0], norm_gain, visible, units, w_query[0], w_output[0], w_keyvalue[0]
    )
    grad_q, grad_out, grad_kv = weight_grads(normed, cotangent, attn, d_query, grad_kv)
    return (
        grad_x[None],
        grad_g.reshape(1, D),
        grad_q[None],
        grad_out[None],
        grad_kv[None],
        grad_image,
    )


def solution(mesh):
    placed = (
        P("section", "mp", None),
        P("section", "mp", None),
        P("section", None),
        P("section", None, "mp"),
        P("section", "mp", None),
        P("section", "mp", None),
        P(("section", "mp"), None),
        P(),
    )
    return jax.shard_map(
        per_device,
        mesh=mesh,
        in_specs=placed,
        out_specs=(
            P("section", "mp", None),
            P("section", None),
            P("section", None, "mp"),
            P("section", "mp", None),
            P("section", "mp", None),
            P(("section", "mp"), None),
        ),
        check_vma=False,
    )
```

```python
import jax
import jax.numpy as jnp
from jax import lax
from jax.experimental import pallas as pl
from jax.experimental.pallas import tpu as pltpu
from jax.sharding import PartitionSpec as P

MESH = pl.DeviceIdType.MESH
F32 = jnp.float32
BF16 = jnp.bfloat16
TOK = 256
D = 8192
HALF = D // 2
QUART = D // 4
CHUNK = 1024
HD = 128
VCOLS = 240
SCALE = HD ** (-0.5)
NSEM = 224

NT = (((1,), (1,)), ((), ()))
TN = (((0,), (0,)), ((), ()))


def dot(a, b, dims=(((1,), (0,)), ((), ()))):
    return lax.dot_general(a, b, dims, preferred_element_type=F32)


class Links:
    def __init__(self, send_sems, recv_sems):
        self.s = lax.axis_index("section")
        index = lax.axis_index("mp")
        self.z, self.x, self.y = index // 8, (index // 4) % 2, index % 4
        self.send_sems, self.recv_sems = send_sems, recv_sems
        self.copies = []

    def coord(self, axis, d):
        if axis == "x":
            return (self.x + d) % 2
        return (getattr(self, axis) + d) % 4

    def peer(self, axis, d):
        at = {"s": self.s, "z": self.z, "x": self.x, "y": self.y}
        at[axis] = self.coord(axis, d)
        return (at["s"], at["z"] * 8 + at["x"] * 4 + at["y"])

    def barrier(self):
        sem = pltpu.get_barrier_semaphore()
        peers = [(a, d) for a in ("z", "y", "s") for d in (1, 2, 3)] + [("x", 1)]
        for a, d in peers:
            pl.semaphore_signal(sem, inc=1, device_id=self.peer(a, d), device_id_type=MESH)
        return lambda: pl.semaphore_wait(sem, len(peers))

    def send(self, axis, d, src, dst):
        at = len(self.copies)
        copy = pltpu.make_async_remote_copy(
            src_ref=src,
            dst_ref=dst,
            send_sem=self.send_sems.at[at],
            recv_sem=self.recv_sems.at[at],
            device_id=self.peer(axis, d),
            device_id_type=MESH,
        )
        copy.start()
        self.copies.append(copy)
        return copy

    def ring(self, axis, src, dst):
        return [self.send(axis, d, src(d), dst(d)) for d in (1, 3, 2)]

    def finish(self):
        assert len(self.copies) <= NSEM
        for copy in self.copies:
            copy.wait_send()


def arrive(copies):
    for copy in copies:
        copy.wait_recv()


class Gather:
    def __init__(self, net, at, first, second, start, size):
        self.net, self.at, self.first, self.second = net, at, first, second
        self.cols = pl.ds(start, size)
        self.sub = (pl.ds(start, size // 2), pl.ds(start + size // 2, size // 2))

    def block(self, i, j, cols):
        i, j = self.net.coord(self.first, i), self.net.coord(self.second, j)
        return self.at(i, j, cols) if self.first == "z" else self.at(j, i, cols)

    def push(self, axis, d, i, j, cols):
        block = self.block(i, j, cols)
        return self.net.send(axis, d, block, block)

    def start(self):
        self.near = [self.push(self.first, d, 0, 0, self.cols) for d in (1, 3)]
        self.lines = [[self.push(self.second, d, 0, 0, self.cols) for d in (1, 3)]]

    def middle(self):
        self.far = []
        for copy, d, sub in zip(self.near, (1, 3), self.sub):
            copy.wait_recv()
            self.far.append(self.push(self.first, d, 4 - d, 0, sub))
            self.lines.append([self.push(self.second, e, 4 - d, 0, self.cols) for e in (1, 3)])

    def spread(self):
        arrive(self.far)
        self.lines.append([self.push(self.second, e, 2, 0, self.cols) for e in (1, 3)])

    def forward(self):
        self.last = []
        for i, line in zip((0, 3, 1, 2), self.lines):
            for copy, d, sub in zip(line, (1, 3), self.sub):
                copy.wait_recv()
                self.last.append(self.push(self.second, d, i, 4 - d, sub))

    def end(self):
        arrive(self.last)


def columns(start, stop, body, step=CHUNK):
    @pl.loop(0, (stop - start) // step)
    def _(i):
        body(pl.ds(pl.multiple_of(start + i * step, step), step))


def layer_kernel(
    tok_ref, cot_ref, gain_ref, vis_ref, unit_ref, wq_hbm, wo_hbm, wkv_hbm,
    n_out, c_out, attn_out, dq_out, gkv_out, gx_out, gg_out, gi_out,
    n_all, c_all, n_t, wq, wo, wkv,
    u_y, u_z, u_x, feat_all,
    fold_n, fold_c, from_n, from_c,
    feat_t, pk, pv, kx, ks0, ks1, ks2, ks3, v_y, v_z, vs1, vs2, vs3, vx, keys, values,
    dk, dv, rk, rv, dkg, dvg,
    pd, via_a, via_b, relay_a, relay_b, near_a, near_b, sa1, sb1, da2, db2, own_d, fold_d, from_d,
    df, dfr, img_s, img_z, img_x, gi_all, gain_part, gz, gy, gx2,
    send_sems, recv_sems, local_sems,
):
    net = Links(send_sems, recv_sems)
    s, z, x, y = net.s, net.z, net.x, net.y
    ready = net.barrier()
    loads = []
    wkv[VCOLS:, :] = jnp.zeros((256 - VCOLS, 2048), BF16)
    for i, (src, dst) in enumerate(((wkv_hbm, wkv.at[:VCOLS]), (wq_hbm, wq), (wo_hbm, wo))):
        copy = pltpu.make_async_copy(src, dst, local_sems.at[i])
        copy.start()
        loads.append(copy)
    xf = tok_ref[...].astype(F32)
    rinv = lax.rsqrt(jnp.mean(xf * xf, axis=-1, keepdims=True) + 1e-05)

    def normed_at(cols):
        return tok_ref[:, cols].astype(F32) * rinv * gain_ref[:, cols]

    def fold_step(at, into):
        def step(i):
            lo = pl.ds(pl.multiple_of(i * CHUNK, CHUNK), CHUNK)
            hi = pl.ds(pl.multiple_of(HALF + i * CHUNK, CHUNK), CHUNK)
            into[:, lo] = jnp.concatenate([at(lo), at(hi)], axis=0).astype(BF16)

        pl.loop(0, HALF // CHUNK)(step)

    fold_step(normed_at, fold_n)
    ready()
    x_n = net.send("x", 1, fold_n, from_n)
    u_y[y] = unit_ref[:, :, y]
    u_1 = net.ring("y", lambda d: unit_ref.at[:, :, net.coord("y", d)], lambda d: u_y.at[y])
    fold_step(lambda cols: cot_ref[:, cols].astype(F32), fold_c)
    x_c = net.send("x", 1, fold_c, from_c)
    arrive(u_1)
    u_z[z] = u_y[:, z]
    u_2 = net.ring("z", lambda d: u_y.at[:, net.coord("z", d)], lambda d: u_z.at[z])

    def unfold(folded, received, full):
        def step(i):
            lo = pl.ds(pl.multiple_of(i * CHUNK, CHUNK), CHUNK)
            hi = pl.ds(pl.multiple_of(HALF + i * CHUNK, CHUNK), CHUNK)
            mine = folded[:, lo].astype(F32)
            other = received[:, lo].astype(F32)
            for at, cols in ((0, lo), (8, hi)):
                a, b = mine[at : at + 8], other[at : at + 8]
                first = jnp.where(x == 0, a, b)
                second = jnp.where(x == 0, b, a)
                full[z, y, :, cols] = jnp.concatenate([first, second], axis=0).astype(BF16)

        pl.loop(0, HALF // CHUNK)(step)

    a_cols, b_cols = pl.ds(0, HALF), pl.ds(HALF, HALF)
    def gathers(full):
        at = lambda i, j, cols: full.at[i, j, :, cols]
        return [Gather(net, at, "z", "y", 0, HALF), Gather(net, at, "y", "z", HALF, HALF)]

    gather_n, gather_c = gathers(n_all), gathers(c_all)
    x_n.wait_recv()
    unfold(fold_n, from_n, n_all)
    for half in gather_n:
        half.start()

    arrive(u_2)
    u_x[x] = u_z[:, :, x]
    u_3 = net.send("x", 1, u_z.at[:, :, 1 - x], u_x.at[x])
    x_c.wait_recv()
    unfold(fold_c, from_c, c_all)
    for half in gather_n:
        half.middle()

    u_3.wait_recv()
    units = u_x[...].reshape(256, HD).astype(BF16)
    row = lax.broadcasted_iota(jnp.int32, (128, 256), 0)
    col = lax.broadcasted_iota(jnp.int32, (128, 256), 1)
    at = (((row // 16) % 2 * 4 + row // 32) * 4 + (row // 4) % 4) * 8 + row % 4
    for half in range(2):
        pick = jnp.where(col == at + 4 * half, 1.0, 0.0).astype(BF16)
        feat_all[s, :, half * HD : (half + 1) * HD] = dot(pick, units).astype(BF16)
    f_0 = net.ring("s", lambda d: feat_all.at[s], lambda d: feat_all.at[s])
    for half in gather_n:
        half.spread()
    arrive(f_0)

    loads[0].wait()

    def kv_step(h):
        cols = pl.ds(pl.multiple_of(h * HD, HD), HD)
        vcols = pl.ds(pl.multiple_of(1024 + h * HD, HD), HD)
        feats = feat_all[...].reshape(512, 256)
        pk[h // 2, h % 2] = dot(feats, wkv[:, cols]).reshape(4, 128, HD)
        pv[h // 2, h % 2] = dot(feats, wkv[:, vcols]).astype(BF16).reshape(4, 128, HD)

    pl.loop(0, 8)(kv_step)

    axes = (("y", "z"), ("z", "y"))
    halves = [pl.ds(0, 64), pl.ds(64, 64)]

    def along(n, level, ref, d):
        axis = axes[n][level]
        at = net.coord(axis, d)
        return ref.at[:, at] if level == 0 and n == 0 else ref.at[at]

    k_x = [net.send("x", 1, pk.at[:, 1 - x, :, rows], kx.at[n]) for n, rows in enumerate(halves)]
    v_1 = [
        net.ring("y", lambda d: pv.at[:, :, net.coord("y", d), halves[0]], lambda d: v_y.at[d - 1]),
        net.ring("z", lambda d: pv.at[net.coord("z", d), :, :, halves[1]], lambda d: v_z.at[d - 1]),
    ]
    for half in gather_n:
        half.forward()
    for half in gather_c:
        half.start()

    v_2 = []
    for n in range(2):
        arrive(v_1[n])
        for a in range(4):
            for b in range(2):
                total = (pv[a, b, y, halves[0]] if n == 0 else pv[z, b, a, halves[1]]).astype(F32)
                for d in range(3):
                    total += (v_y[d, a, b] if n == 0 else v_z[d, b, a]).astype(F32)
                vs1[n, a, b] = total
        v_2.append(
            net.ring(axes[n][1], lambda d: along(n, 1, vs1.at[n], d), lambda d: vs2.at[n, d - 1])
        )
    for half in gather_c:
        half.middle()
    k_2 = []
    for n, rows in enumerate(halves):
        k_x[n].wait_recv()
        for a in range(4):
            ks0[n, a] = pk[a, x, :, rows] + kx[n, a]
        k_2.append(
            net.ring(axes[n][0], lambda d: along(n, 0, ks0.at[n], d), lambda d: ks1.at[n, d - 1])
        )
    v_x = []
    for n in range(2):
        arrive(v_2[n])
        mine = net.coord(axes[n][1], 0)
        for b in range(2):
            total = vs1[n, mine, b]
            for d in range(3):
                total += vs2[n, d, b]
            vs3[n, b] = total
        v_x.append(net.send("x", 1, vs3.at[n, 1 - x], vx.at[n]))
    for half in gather_c:
        half.spread()
    k_3 = []
    for n in range(2):
        arrive(k_2[n])
        for a in range(4):
            total = ks0[n, a, y] if n == 0 else ks0[n, z, a]
            for d in range(3):
                total += ks1[n, d, a]
            ks2[n, a] = total
        k_3.append(
            net.ring(axes[n][1], lambda d: along(n, 1, ks2.at[n], d), lambda d: ks3.at[n, d - 1])
        )
    for n in range(2):
        v_x[n].wait_recv()
        values[y, 64 * n : 64 * n + 64] = (vs3[n, x] + vx[n]).astype(BF16)
    v_3 = net.ring("y", lambda d: values.at[y], lambda d: values.at[y])
    for n in range(2):
        arrive(k_3[n])
        total = ks2[n, net.coord(axes[n][1], 0)]
        for d in range(3):
            total += ks3[n, d]
        keys[y, 64 * n : 64 * n + 64] = total.astype(BF16)
    k_3 = net.ring("y", lambda d: keys.at[y], lambda d: keys.at[y])

    for half in gather_n:
        half.end()
    loads[1].wait()

    def query_step(i, acc):
        cols = pl.ds(pl.multiple_of(i * CHUNK, CHUNK), CHUNK)
        return acc + dot(n_all[:, :, :, cols].reshape(TOK, CHUNK), wq[cols, :])

    query = lax.fori_loop(0, D // CHUNK, query_step, jnp.zeros((TOK, 256), F32)).astype(BF16)

    for half in gather_c:
        half.forward()
    stores = []
    arrive(k_3)
    arrive(v_3)
    key = keys[...].reshape(512, HD)
    value = values[...].reshape(512, HD)
    image_of = lax.broadcasted_iota(jnp.int32, (TOK, 512), 1) // 128
    late = lax.broadcasted_iota(jnp.int32, (TOK, 512), 0) >= 128
    allowed = image_of < jnp.where(late, vis_ref[1], vis_ref[0])
    probs, weights = [], []
    for j in range(2):
        q = query[:, j * HD : (j + 1) * HD]
        scores = jnp.where(allowed, dot(q, key, NT) * SCALE, -1e30)
        expo = jnp.exp(scores - jnp.max(scores, axis=-1, keepdims=True))
        prob = expo / jnp.sum(expo, axis=-1, keepdims=True)
        probs.append(prob)
        weights.append(prob.astype(BF16))
        attn = dot(weights[j], value).astype(BF16)
        attn_out[j * HD : (j + 1) * HD, :] = attn.astype(F32).T.astype(BF16)

    for half in gather_c:
        half.end()
    copy = pltpu.make_async_copy(c_all, c_out, local_sems.at[4])
    copy.start()
    stores.append(copy)
    loads[2].wait()

    def d_attn_step(i, acc):
        cols = pl.ds(pl.multiple_of(i * CHUNK, CHUNK), CHUNK)
        return acc + dot(c_all[:, :, :, cols].reshape(TOK, CHUNK), wo[:, cols], NT)

    d_attn = lax.fori_loop(0, D // CHUNK, d_attn_step, jnp.zeros((TOK, 256), F32)).astype(BF16)
    d_key = jnp.zeros((512, HD), F32)
    d_value = jnp.zeros((512, HD), F32)
    for j in range(2):
        heads = slice(j * HD, (j + 1) * HD)
        da = d_attn[:, heads]
        d_prob = dot(da, value, NT)
        delta = jnp.sum(probs[j] * d_prob, axis=-1, keepdims=True)
        d_score = (probs[j] * (d_prob - delta) * SCALE).astype(BF16)
        dq_out[:, heads] = dot(d_score, key).astype(BF16)
        d_key += dot(d_score, query[:, heads], TN)
        d_value += dot(weights[j], da, TN)
    dk[...] = d_key.astype(BF16).reshape(4, 128, HD)
    dv[...] = d_value.astype(BF16).reshape(4, 128, HD)
    dk_1 = net.ring("y", lambda d: dk.at[net.coord("y", d)], lambda d: rk.at[d - 1])
    dv_1 = net.ring("y", lambda d: dv.at[net.coord("y", d)], lambda d: rv.at[d - 1])

    def d_normed_step(cols):
        part = dot(dq_out[...], wq[cols, :], NT)
        pd[:, :, :, cols] = part.astype(BF16).reshape(4, 4, 16, CHUNK)

    def gain_step(cols):
        part = pd[:, :, :, cols].reshape(TOK, CHUNK).astype(F32)
        normed = n_all[:, :, :, cols].reshape(TOK, CHUNK).astype(F32)
        gain_part[:, cols] = jnp.sum(part * normed, axis=0, keepdims=True) / gain_ref[:, cols]

    def line(axis, d, cols):
        at = net.coord(axis, d)
        return pd.at[:, at, :, cols] if axis == "y" else pd.at[at, :, :, cols]

    def reduce_far(axis, start, via):
        return [
            net.send(axis, d, line(axis, 2, pl.ds(start + n * QUART, QUART)), via.at[n])
            for n, d in enumerate((1, 3))
        ]

    def reduce_near(axis, start, near):
        out = []
        for n, d in enumerate((1, 3)):
            block = line(axis, d, pl.ds(start + (1 - n) * QUART, QUART))
            out.append(net.send(axis, d, block, near.at[n, :, :, pl.ds((1 - n) * QUART, QUART)]))
        return out

    def reduce_on(axis, start, via, relay, near, far):
        out = []
        for n, d in enumerate((1, 3)):
            far[n].wait_recv()
            at = net.coord(axis, d)

            def step(i):
                cols = pl.ds(pl.multiple_of(i * CHUNK, CHUNK), CHUNK)
                own = pl.ds(pl.multiple_of(start + n * QUART + i * CHUNK, CHUNK), CHUNK)
                mine = pd[:, at, :, own] if axis == "y" else pd[at, :, :, own]
                relay[n, :, :, cols] = (mine.astype(F32) + via[n, :, :, cols].astype(F32)).astype(BF16)

            pl.loop(0, QUART // CHUNK)(step)
            out.append(net.send(axis, d, relay.at[n], near.at[n, :, :, pl.ds(n * QUART, QUART)]))
        return out

    def reduce_end(axis, start, near, copies, into):
        arrive(copies)

        def step(i):
            cols = pl.ds(pl.multiple_of(i * CHUNK, CHUNK), CHUNK)
            own = pl.ds(pl.multiple_of(start + i * CHUNK, CHUNK), CHUNK)
            total = (pd[:, y, :, own] if axis == "y" else pd[z, :, :, own]).astype(F32)
            into[:, :, cols] = (
                total + near[0, :, :, cols].astype(F32) + near[1, :, :, cols].astype(F32)
            ).astype(BF16)

        pl.loop(0, HALF // CHUNK)(step)

    columns(0, HALF, d_normed_step)
    da_far = reduce_far("y", 0, via_a)
    columns(HALF, D, d_normed_step)
    db_far = reduce_far("z", HALF, via_b)
    arrive(dk_1)
    arrive(dv_1)
    total = dk[y].astype(F32)
    vtotal = dv[y].astype(F32)
    for d in range(3):
        total += rk[d].astype(F32)
        vtotal += rv[d].astype(F32)
    dkg[z, x, y] = total.astype(BF16)
    dvg[z, x, y] = vtotal.astype(BF16)
    mine_k, mine_v = dkg.at[z, x, y], dvg.at[z, x, y]
    dk_2 = net.send("x", 1, mine_k, mine_k)
    dv_2 = net.send("x", 1, mine_v, mine_v)
    gather_d = [
        Gather(net, lambda i, j, rows: dkg.at[i, :, j, rows], "z", "y", 0, HD),
        Gather(net, lambda i, j, rows: dvg.at[i, :, j, rows], "y", "z", 0, HD),
    ]
    dk_2.wait_recv()
    dv_2.wait_recv()
    for part in gather_d:
        part.start()
    columns(0, D, gain_step)
    for i in range(8):
        gz[z, i : i + 1, :] = gain_part[:, i * 1024 : (i + 1) * 1024]
    g_1 = net.ring("z", lambda d: gz.at[z], lambda d: gz.at[z])

    for part in gather_d:
        part.middle()
    da_near = reduce_on("y", 0, via_a, relay_a, near_a, da_far)
    for part in gather_d:
        part.spread()
    db_near = reduce_on("z", HALF, via_b, relay_b, near_b, db_far)
    for part in gather_d:
        part.forward()
    da_near += reduce_near("y", 0, near_a)
    db_near += reduce_near("z", HALF, near_b)
    feat_t[...] = feat_all[...].reshape(512, 256).astype(F32).T.astype(BF16)

    def turn_step(i):
        cols = pl.ds(pl.multiple_of(i * CHUNK, CHUNK), CHUNK)
        n_t[cols, :] = n_all[:, :, :, cols].reshape(TOK, CHUNK).astype(F32).T.astype(BF16)

    pl.loop(0, D // CHUNK)(turn_step)
    copy = pltpu.make_async_copy(n_t, n_out, local_sems.at[3])
    copy.start()
    stores.append(copy)
    arrive(g_1)
    gy[y] = (gz[0] + gz[1]) + (gz[2] + gz[3])
    g_2 = net.ring("y", lambda d: gy.at[y], lambda d: gy.at[y])

    for part in gather_d:
        part.end()
    d_feats = jnp.zeros((512, 256), F32)
    for h in range(8):
        both = jnp.concatenate(
            [full[h // 2, h % 2].reshape(512, HD) for full in (dkg, dvg)], axis=1
        )
        weights_h = jnp.concatenate(
            [wkv[:, at : at + HD] for at in (h * HD, 1024 + h * HD)], axis=1
        )
        d_feats += dot(both, weights_h, NT)
    df[...] = d_feats.astype(BF16).reshape(4, 128, 256)
    f_1 = net.ring("s", lambda d: df.at[net.coord("s", d)], lambda d: dfr.at[d - 1])
    reduce_end("y", 0, near_a, da_near, sa1)
    da_2 = net.ring("z", lambda d: sa1.at[net.coord("z", d)], lambda d: da2.at[d - 1])
    reduce_end("z", HALF, near_b, db_near, sb1)
    db_2 = net.ring("y", lambda d: sb1.at[net.coord("y", d)], lambda d: db2.at[d - 1])
    arrive(f_1)
    img = df[s].astype(F32)
    for d in range(3):
        img += dfr[d].astype(F32)
    img_s[...] = img.reshape(4, 32, 256)
    img_z[z] = img_s[z]
    f_2 = net.ring("z", lambda d: img_s.at[net.coord("z", d)], lambda d: img_z.at[z])
    for h in range(8):
        for at, full in ((h * HD, dkg), (1024 + h * HD, dvg)):
            gkv_out[:, at : at + HD] = dot(feat_t[...], full[h // 2, h % 2].reshape(512, HD)).astype(BF16)
    arrive(g_2)
    gx2[x] = (gy[0] + gy[1]) + (gy[2] + gy[3])
    g_3 = net.send("x", 1, gx2.at[x], gx2.at[x])

    arrive(f_2)
    img_x[x] = img_z[:, pl.ds(pl.multiple_of(x * 16, 16), 16), :]
    far = pl.ds(pl.multiple_of((1 - x) * 16, 16), 16)
    f_3 = net.send("x", 1, img_z.at[:, far], img_x.at[x])
    arrive(da_2)
    arrive(db_2)

    def sum_ab(i):
        cols = pl.ds(pl.multiple_of(i * CHUNK, CHUNK), CHUNK)
        ta = sa1[z, :, cols].astype(F32)
        tb = sb1[y, :, cols].astype(F32)
        for d in range(3):
            ta += da2[d, :, cols].astype(F32)
            tb += db2[d, :, cols].astype(F32)
        own_d[:8, cols] = jnp.where(x == 0, ta[:8], ta[8:])
        own_d[8:, cols] = jnp.where(x == 0, tb[:8], tb[8:])
        fold_d[:, cols] = jnp.concatenate(
            [jnp.where(x == 0, ta[8:], ta[:8]), jnp.where(x == 0, tb[8:], tb[:8])], axis=0
        ).astype(BF16)

    pl.loop(0, HALF // CHUNK)(sum_ab)
    d_x = net.send("x", 1, fold_d, from_d)

    f_3.wait_recv()

    def tile(d):
        return pl.ds(pl.multiple_of((net.coord("y", d) // 2) * 8, 8), 8)

    gi_all[y] = img_x[:, :, tile(0), :]
    f_4 = net.ring("y", lambda d: img_x.at[:, :, tile(d)], lambda d: gi_all.at[y])
    g_3.wait_recv()
    gain = gx2[0] + gx2[1]
    for i in range(8):
        gg_out[:, i * 1024 : (i + 1) * 1024] = gain[i : i + 1]
    d_x.wait_recv()
    both = own_d[...] + from_d[...].astype(F32)
    dn = jnp.concatenate([both[:8], both[8:]], axis=1)
    xf = tok_ref[...].astype(F32)
    scaled = dn * gain_ref[...]
    gx_out[...] = (
        rinv * scaled - xf * rinv * rinv * rinv * jnp.mean(xf * scaled, axis=-1, keepdims=True)
    ).astype(BF16)
    arrive(f_4)
    for m in range(32):
        tile_m = gi_all[m % 4, (m // 4) % 2, m // 8]
        gi_out[:, m * VCOLS : (m + 1) * VCOLS] = jnp.where(y % 2 == 0, tile_m[:4], tile_m[4:])[:, :VCOLS]
    for copy in stores:
        copy.wait()
    net.finish()


def run_layer(tokens, cotangent, gain_row, visible, units, w_q, w_o, w_kv):
    any_spec = pl.BlockSpec(memory_space=pl.ANY)
    vmem = pl.BlockSpec(memory_space=pltpu.VMEM)
    smem = pl.BlockSpec(memory_space=pltpu.SMEM)
    shape = jax.ShapeDtypeStruct
    b, f = (lambda *dims: pltpu.VMEM(dims, BF16)), (lambda *dims: pltpu.VMEM(dims, F32))
    return pl.pallas_call(
        layer_kernel,
        out_shape=(
            shape((D, 256), BF16),
            shape((4, 4, 16, D), BF16),
            shape((TOK, 256), BF16),
            shape((TOK, 256), BF16),
            shape((256, 2048), BF16),
            shape((8, D), BF16),
            shape((1, D), F32),
            shape((4, 32 * VCOLS), F32),
        ),
        in_specs=[vmem, vmem, vmem, smem, vmem, any_spec, any_spec, any_spec],
        out_specs=(any_spec, any_spec, vmem, vmem, vmem, vmem, vmem, vmem),
        scratch_shapes=[
            b(4, 4, 16, D), b(4, 4, 16, D), b(D, 256), b(D, 256), b(256, D), b(256, 2048),
            f(4, 4, 2, 8, HD), f(4, 4, 2, 8, HD), f(2, 4, 4, 8, HD), b(4, 128, 256),
            b(16, HALF), b(16, HALF), b(16, HALF), b(16, HALF),
            b(256, 512), f(4, 2, 4, 128, HD), b(4, 2, 4, 128, HD),
            f(2, 4, 4, 64, HD), f(2, 4, 4, 64, HD), f(2, 3, 4, 64, HD),
            f(2, 4, 64, HD), f(2, 3, 64, HD),
            b(3, 4, 2, 64, HD), b(3, 2, 4, 64, HD), f(2, 4, 2, 64, HD), f(2, 3, 2, 64, HD),
            f(2, 2, 64, HD), f(2, 64, HD),
            b(4, 128, HD), b(4, 128, HD),
            b(4, 128, HD), b(4, 128, HD), b(3, 128, HD), b(3, 128, HD),
            b(4, 2, 4, 128, HD), b(4, 2, 4, 128, HD),
            b(4, 4, 16, D),
            b(2, 4, 16, QUART), b(2, 4, 16, QUART), b(2, 4, 16, QUART), b(2, 4, 16, QUART),
            b(2, 4, 16, HALF), b(2, 4, 16, HALF),
            b(4, 16, HALF), b(4, 16, HALF),
            b(3, 16, HALF), b(3, 16, HALF),
            f(16, HALF), b(16, HALF), b(16, HALF),
            b(4, 128, 256), b(3, 128, 256),
            f(4, 32, 256), f(4, 32, 256), f(2, 4, 16, 256), f(4, 2, 4, 8, 256),
            f(1, D), f(4, 8, 1024), f(4, 8, 1024), f(2, 8, 1024),
            pltpu.SemaphoreType.DMA((NSEM,)),
            pltpu.SemaphoreType.DMA((NSEM,)),
            pltpu.SemaphoreType.DMA((5,)),
        ],
        compiler_params=pltpu.CompilerParams(
            collective_id=0, has_side_effects=True, vmem_limit_bytes=58 * 1024 * 1024
        ),
        cost_estimate=pl.CostEstimate(
            flops=6 * 10**9, bytes_accessed=20 * 2**20, transcendentals=2 * 256 * 512
        ),
        name="layer",
    )(tokens, cotangent, gain_row, visible, units, w_q, w_o, w_kv)


def weight_kernel(nt_ref, c_ref, at_ref, dq_ref, gkv_ref, gx_ref, gg_ref, gi_ref, *outs):
    gq_out, go_out, gk_out, gx_out, gg_out, gi_out = outs
    gq_out[...] = dot(nt_ref[...], dq_ref[...]).astype(BF16)
    go_out[...] = dot(at_ref[...], c_ref[...].reshape(TOK, c_ref.shape[-1])).astype(BF16)
    gk_out[...] = gkv_ref[:VCOLS, :]
    gx_out[...] = gx_ref[...]
    gg_out[...] = gg_ref[...]
    gi_out[...] = gi_ref[...]


def weight_grads(normed_t, cotangent, attn_t, d_query, grad_kv, grad_x, grad_g, grad_image):
    steps = 4
    width, kv_width, im_width = D // steps, 2048 // steps, 32 * VCOLS // steps
    shape = jax.ShapeDtypeStruct
    whole = pl.BlockSpec((TOK, 256), lambda i: (0, 0))

    def by_column(rows, cols):
        return pl.BlockSpec((rows, cols), lambda i: (0, i))

    return pl.pallas_call(
        weight_kernel,
        grid=(steps,),
        out_shape=(
            shape((D, 256), BF16),
            shape((256, D), BF16),
            shape((VCOLS, 2048), BF16),
            shape((8, D), BF16),
            shape((1, D), F32),
            shape((4, 32 * VCOLS), F32),
        ),
        in_specs=[
            pl.BlockSpec((width, 256), lambda i: (i, 0)),
            pl.BlockSpec((4, 4, 16, width), lambda i: (0, 0, 0, i)),
            whole,
            whole,
            by_column(256, kv_width),
            by_column(8, width),
            by_column(1, width),
            by_column(4, im_width),
        ],
        out_specs=(
            pl.BlockSpec((width, 256), lambda i: (i, 0)),
            by_column(256, width),
            by_column(VCOLS, kv_width),
            by_column(8, width),
            by_column(1, width),
            by_column(4, im_width),
        ),
        compiler_params=pltpu.CompilerParams(vmem_limit_bytes=62 * 1024 * 1024),
        name="weight_grads",
    )(normed_t, cotangent, attn_t, d_query, grad_kv, grad_x, grad_g, grad_image)


def per_device(tokens, upstream, norm_gain, w_query, w_output, w_keyvalue, image_feats, visible):
    units = image_feats.astype(F32).reshape(4, 32, VCOLS)
    units = jnp.pad(units, ((0, 0), (0, 0), (0, 256 - VCOLS))).reshape(4, 32, 2, HD)
    units = units.transpose(1, 2, 0, 3).reshape(4, 2, 4, 8, HD)
    results = run_layer(
        tokens[0], upstream[0], norm_gain, visible, units, w_query[0], w_output[0], w_keyvalue[0]
    )
    grad_q, grad_out, grad_kv, grad_x, grad_g, grad_image = weight_grads(*results)
    return (grad_x[None], grad_g, grad_q[None], grad_out[None], grad_kv[None], grad_image)


def solution(mesh):
    placed = (
        P("section", "mp", None),
        P("section", "mp", None),
        P("section", None),
        P("section", None, "mp"),
        P("section", "mp", None),
        P("section", "mp", None),
        P(("section", "mp"), None),
        P(),
    )
    return jax.shard_map(
        per_device,
        mesh=mesh,
        in_specs=placed,
        out_specs=(
            P("section", "mp", None),
            P("section", None),
            P("section", None, "mp"),
            P("section", "mp", None),
            P("section", "mp", None),
            P(("section", "mp"), None),
        ),
        check_vma=False,
    )
```

```python
import jax
import jax.numpy as jnp
from jax import lax
from jax.experimental import pallas as pl
from jax.experimental.pallas import tpu as pltpu
from jax.sharding import PartitionSpec as P

MESH = pl.DeviceIdType.MESH
F32 = jnp.float32
BF16 = jnp.bfloat16
TOK = 256
D = 8192
HALF = D // 2
QUART = D // 4
CHUNK = 1024
HD = 128
VCOLS = 240
SCALE = HD ** (-0.5)
NSEM = 224

NT = (((1,), (1,)), ((), ()))
TN = (((0,), (0,)), ((), ()))


def dot(a, b, dims=(((1,), (0,)), ((), ()))):
    return lax.dot_general(a, b, dims, preferred_element_type=F32)


class Links:
    def __init__(self, send_sems, recv_sems):
        self.s = lax.axis_index("section")
        index = lax.axis_index("mp")
        self.z, self.x, self.y = index // 8, (index // 4) % 2, index % 4
        self.send_sems, self.recv_sems = send_sems, recv_sems
        self.copies = []

    def coord(self, axis, d):
        if axis == "x":
            return (self.x + d) % 2
        return (getattr(self, axis) + d) % 4

    def peer(self, axis, d):
        at = {"s": self.s, "z": self.z, "x": self.x, "y": self.y}
        at[axis] = self.coord(axis, d)
        return (at["s"], at["z"] * 8 + at["x"] * 4 + at["y"])

    def barrier(self):
        sem = pltpu.get_barrier_semaphore()
        peers = [(a, d) for a in ("z", "y", "s") for d in (1, 2, 3)] + [("x", 1)]
        for a, d in peers:
            pl.semaphore_signal(sem, inc=1, device_id=self.peer(a, d), device_id_type=MESH)
        return lambda: pl.semaphore_wait(sem, len(peers))

    def send(self, axis, d, src, dst):
        at = len(self.copies)
        copy = pltpu.make_async_remote_copy(
            src_ref=src,
            dst_ref=dst,
            send_sem=self.send_sems.at[at],
            recv_sem=self.recv_sems.at[at],
            device_id=self.peer(axis, d),
            device_id_type=MESH,
        )
        copy.start()
        self.copies.append(copy)
        return copy

    def ring(self, axis, src, dst):
        return [self.send(axis, d, src(d), dst(d)) for d in (1, 3, 2)]

    def finish(self):
        assert len(self.copies) <= NSEM
        for copy in self.copies:
            copy.wait_send()


def arrive(copies):
    for copy in copies:
        copy.wait_recv()


class Gather:
    def __init__(self, net, at, first, second, start, size):
        self.net, self.at, self.first, self.second = net, at, first, second
        self.cols = pl.ds(start, size)
        self.sub = (pl.ds(start, size // 2), pl.ds(start + size // 2, size // 2))

    def block(self, i, j, cols):
        i, j = self.net.coord(self.first, i), self.net.coord(self.second, j)
        return self.at(i, j, cols) if self.first == "z" else self.at(j, i, cols)

    def push(self, axis, d, i, j, cols):
        block = self.block(i, j, cols)
        return self.net.send(axis, d, block, block)

    def start(self):
        self.near = [self.push(self.first, d, 0, 0, self.cols) for d in (1, 3)]
        self.lines = [[self.push(self.second, d, 0, 0, self.cols) for d in (1, 3)]]

    def middle(self):
        self.far = []
        for copy, d, sub in zip(self.near, (1, 3), self.sub):
            copy.wait_recv()
            self.far.append(self.push(self.first, d, 4 - d, 0, sub))
            self.lines.append([self.push(self.second, e, 4 - d, 0, self.cols) for e in (1, 3)])

    def spread(self):
        arrive(self.far)
        self.lines.append([self.push(self.second, e, 2, 0, self.cols) for e in (1, 3)])

    def forward(self):
        self.last = []
        for i, line in zip((0, 3, 1, 2), self.lines):
            for copy, d, sub in zip(line, (1, 3), self.sub):
                copy.wait_recv()
                self.last.append(self.push(self.second, d, i, 4 - d, sub))

    def end(self):
        arrive(self.last)


def columns(start, stop, body, step=CHUNK):
    @pl.loop(0, (stop - start) // step)
    def _(i):
        body(pl.ds(pl.multiple_of(start + i * step, step), step))


def layer_kernel(
    tok_ref, cot_ref, gain_ref, vis_ref, feat_ref, wq_hbm, wo_hbm, wkv_hbm,
    n_out, c_out, attn_hbm, dq_hbm, gkv_hbm, gx_out, gg_out, gi_out,
    attn_out, dq_out, gkv_out,
    n_all, c_all, n_t, wq, wo, wkv,
    unit_ref, u_y, u_z, u_x, feat_all,
    fold_n, fold_c, from_n, from_c,
    feat_t, pk, pv, kx, ks0, ks1, ks2, ks3, v_y, v_z, vs1, vs2, vs3, vx, keys, values,
    dk, dv, rk, rv, dkg, dvg,
    pd, via_a, via_b, relay_a, relay_b, near_a, near_b, sa1, sb1, da2, db2, own_d, fold_d, from_d,
    df, dfr, img_s, img_z, img_x, gi_all, gain_part, gz, gy, gx2,
    send_sems, recv_sems, local_sems,
):
    net = Links(send_sems, recv_sems)
    s, z, x, y = net.s, net.z, net.x, net.y
    ready = net.barrier()
    loads = []
    wkv[VCOLS:, :] = jnp.zeros((256 - VCOLS, 2048), BF16)
    for i, (src, dst) in enumerate(((wkv_hbm, wkv.at[:VCOLS]), (wq_hbm, wq), (wo_hbm, wo))):
        copy = pltpu.make_async_copy(src, dst, local_sems.at[i])
        copy.start()
        loads.append(copy)
    xf = tok_ref[...].astype(F32)
    rinv = lax.rsqrt(jnp.mean(xf * xf, axis=-1, keepdims=True) + 1e-05)

    def normed_at(cols):
        return tok_ref[:, cols].astype(F32) * rinv * gain_ref[:, cols]

    def fold_step(at, into):
        def step(i):
            lo = pl.ds(pl.multiple_of(i * CHUNK, CHUNK), CHUNK)
            hi = pl.ds(pl.multiple_of(HALF + i * CHUNK, CHUNK), CHUNK)
            into[:, lo] = jnp.concatenate([at(lo), at(hi)], axis=0).astype(BF16)

        pl.loop(0, HALF // CHUNK)(step)

    fold_step(normed_at, fold_n)

    wide = feat_ref[...].astype(F32)
    for m in range(32):
        cols = wide[:, m * VCOLS : (m + 1) * VCOLS]
        rest = jnp.concatenate([cols[:, HD:], jnp.zeros((4, 256 - VCOLS), F32)], axis=1)
        unit_ref[m // 8, (m // 4) % 2, m % 4] = jnp.concatenate([cols[:, :HD], rest], axis=0)
    ready()
    x_n = net.send("x", 1, fold_n, from_n)
    u_y[y] = unit_ref[:, :, y]
    u_1 = net.ring("y", lambda d: unit_ref.at[:, :, net.coord("y", d)], lambda d: u_y.at[y])
    fold_step(lambda cols: cot_ref[:, cols].astype(F32), fold_c)
    x_c = net.send("x", 1, fold_c, from_c)
    arrive(u_1)
    u_z[z] = u_y[:, z]
    u_2 = net.ring("z", lambda d: u_y.at[:, net.coord("z", d)], lambda d: u_z.at[z])

    def unfold(folded, received, full):
        def step(i):
            lo = pl.ds(pl.multiple_of(i * CHUNK, CHUNK), CHUNK)
            hi = pl.ds(pl.multiple_of(HALF + i * CHUNK, CHUNK), CHUNK)
            mine = folded[:, lo].astype(F32)
            other = received[:, lo].astype(F32)
            for at, cols in ((0, lo), (8, hi)):
                a, b = mine[at : at + 8], other[at : at + 8]
                first = jnp.where(x == 0, a, b)
                second = jnp.where(x == 0, b, a)
                full[z, y, :, cols] = jnp.concatenate([first, second], axis=0).astype(BF16)

        pl.loop(0, HALF // CHUNK)(step)

    a_cols, b_cols = pl.ds(0, HALF), pl.ds(HALF, HALF)
    def gathers(full):
        at = lambda i, j, cols: full.at[i, j, :, cols]
        return [Gather(net, at, "z", "y", 0, HALF), Gather(net, at, "y", "z", HALF, HALF)]

    gather_n, gather_c = gathers(n_all), gathers(c_all)
    x_n.wait_recv()
    unfold(fold_n, from_n, n_all)
    for half in gather_n:
        half.start()

    arrive(u_2)
    u_x[x] = u_z[:, :, x]
    u_3 = net.send("x", 1, u_z.at[:, :, 1 - x], u_x.at[x])
    x_c.wait_recv()
    unfold(fold_c, from_c, c_all)
    for half in gather_n:
        half.middle()

    u_3.wait_recv()
    units = u_x[...].reshape(256, HD).astype(BF16)
    row = lax.broadcasted_iota(jnp.int32, (128, 256), 0)
    col = lax.broadcasted_iota(jnp.int32, (128, 256), 1)
    at = (((row // 16) % 2 * 4 + row // 32) * 4 + (row // 4) % 4) * 8 + row % 4
    for half in range(2):
        pick = jnp.where(col == at + 4 * half, 1.0, 0.0).astype(BF16)
        feat_all[s, :, half * HD : (half + 1) * HD] = dot(pick, units).astype(BF16)
    f_0 = net.ring("s", lambda d: feat_all.at[s], lambda d: feat_all.at[s])
    for half in gather_n:
        half.spread()
    arrive(f_0)

    loads[0].wait()

    def kv_step(h):
        cols = pl.ds(pl.multiple_of(h * HD, HD), HD)
        vcols = pl.ds(pl.multiple_of(1024 + h * HD, HD), HD)
        feats = feat_all[...].reshape(512, 256)
        pk[h // 2, h % 2] = dot(feats, wkv[:, cols]).reshape(4, 128, HD)
        pv[h // 2, h % 2] = dot(feats, wkv[:, vcols]).astype(BF16).reshape(4, 128, HD)

    pl.loop(0, 8)(kv_step)

    axes = (("y", "z"), ("z", "y"))
    halves = [pl.ds(0, 64), pl.ds(64, 64)]

    def along(n, level, ref, d):
        axis = axes[n][level]
        at = net.coord(axis, d)
        return ref.at[:, at] if level == 0 and n == 0 else ref.at[at]

    k_x = [net.send("x", 1, pk.at[:, 1 - x, :, rows], kx.at[n]) for n, rows in enumerate(halves)]
    v_1 = [
        net.ring("y", lambda d: pv.at[:, :, net.coord("y", d), halves[0]], lambda d: v_y.at[d - 1]),
        net.ring("z", lambda d: pv.at[net.coord("z", d), :, :, halves[1]], lambda d: v_z.at[d - 1]),
    ]
    for half in gather_n:
        half.forward()
    for half in gather_c:
        half.start()

    v_2 = []
    for n in range(2):
        arrive(v_1[n])
        for a in range(4):
            for b in range(2):
                total = (pv[a, b, y, halves[0]] if n == 0 else pv[z, b, a, halves[1]]).astype(F32)
                for d in range(3):
                    total += (v_y[d, a, b] if n == 0 else v_z[d, b, a]).astype(F32)
                vs1[n, a, b] = total
        v_2.append(
            net.ring(axes[n][1], lambda d: along(n, 1, vs1.at[n], d), lambda d: vs2.at[n, d - 1])
        )
    for half in gather_c:
        half.middle()
    for half in gather_n:
        half.end()
    loads[1].wait()

    def query_step(i, acc):
        cols = pl.ds(pl.multiple_of(i * CHUNK, CHUNK), CHUNK)
        return acc + dot(n_all[:, :, :, cols].reshape(TOK, CHUNK), wq[cols, :])

    query = lax.fori_loop(0, D // CHUNK, query_step, jnp.zeros((TOK, 256), F32)).astype(BF16)
    for half in gather_c:
        half.spread()
    k_2 = []
    for n, rows in enumerate(halves):
        k_x[n].wait_recv()
        for a in range(4):
            ks0[n, a] = pk[a, x, :, rows] + kx[n, a]
        k_2.append(
            net.ring(axes[n][0], lambda d: along(n, 0, ks0.at[n], d), lambda d: ks1.at[n, d - 1])
        )
    v_x = []
    for n in range(2):
        arrive(v_2[n])
        mine = net.coord(axes[n][1], 0)
        for b in range(2):
            total = vs1[n, mine, b]
            for d in range(3):
                total += vs2[n, d, b]
            vs3[n, b] = total
        v_x.append(net.send("x", 1, vs3.at[n, 1 - x], vx.at[n]))
    k_3 = []
    for n in range(2):
        arrive(k_2[n])
        for a in range(4):
            total = ks0[n, a, y] if n == 0 else ks0[n, z, a]
            for d in range(3):
                total += ks1[n, d, a]
            ks2[n, a] = total
        k_3.append(
            net.ring(axes[n][1], lambda d: along(n, 1, ks2.at[n], d), lambda d: ks3.at[n, d - 1])
        )
    for half in gather_c:
        half.forward()
    for n in range(2):
        v_x[n].wait_recv()
        values[y, 64 * n : 64 * n + 64] = (vs3[n, x] + vx[n]).astype(BF16)
    v_3 = net.ring("y", lambda d: values.at[y], lambda d: values.at[y])
    for n in range(2):
        arrive(k_3[n])
        total = ks2[n, net.coord(axes[n][1], 0)]
        for d in range(3):
            total += ks3[n, d]
        keys[y, 64 * n : 64 * n + 64] = total.astype(BF16)
    k_3 = net.ring("y", lambda d: keys.at[y], lambda d: keys.at[y])

    stores = []
    arrive(k_3)
    arrive(v_3)
    key = keys[...].reshape(512, HD)
    value = values[...].reshape(512, HD)
    image_of = lax.broadcasted_iota(jnp.int32, (TOK, 512), 1) // 128
    late = lax.broadcasted_iota(jnp.int32, (TOK, 512), 0) >= 128
    allowed = image_of < jnp.where(late, vis_ref[1], vis_ref[0])
    probs, weights = [], []
    for j in range(2):
        q = query[:, j * HD : (j + 1) * HD]
        scores = jnp.where(allowed, dot(q, key, NT) * SCALE, -1e30)
        expo = jnp.exp(scores - jnp.max(scores, axis=-1, keepdims=True))
        prob = expo / jnp.sum(expo, axis=-1, keepdims=True)
        probs.append(prob)
        weights.append(prob.astype(BF16))
        attn = dot(weights[j], value).astype(BF16)
        attn_out[j * HD : (j + 1) * HD, :] = attn.astype(F32).T.astype(BF16)

    for half in gather_c:
        half.end()
    copy = pltpu.make_async_copy(c_all, c_out, local_sems.at[4])
    copy.start()
    stores.append(copy)
    loads[2].wait()

    def d_attn_step(i, acc):
        cols = pl.ds(pl.multiple_of(i * CHUNK, CHUNK), CHUNK)
        return acc + dot(c_all[:, :, :, cols].reshape(TOK, CHUNK), wo[:, cols], NT)

    d_attn = lax.fori_loop(0, D // CHUNK, d_attn_step, jnp.zeros((TOK, 256), F32)).astype(BF16)
    d_key = jnp.zeros((512, HD), F32)
    d_value = jnp.zeros((512, HD), F32)
    for j in range(2):
        heads = slice(j * HD, (j + 1) * HD)
        da = d_attn[:, heads]
        d_prob = dot(da, value, NT)
        delta = jnp.sum(probs[j] * d_prob, axis=-1, keepdims=True)
        d_score = (probs[j] * (d_prob - delta) * SCALE).astype(BF16)
        dq_out[:, heads] = dot(d_score, key).astype(BF16)
        d_key += dot(d_score, query[:, heads], TN)
        d_value += dot(weights[j], da, TN)
    for i, (src, dst) in enumerate(((attn_out, attn_hbm), (dq_out, dq_hbm))):
        copy = pltpu.make_async_copy(src, dst, local_sems.at[5 + i])
        copy.start()
        stores.append(copy)
    dk[...] = d_key.astype(BF16).reshape(4, 128, HD)
    dv[...] = d_value.astype(BF16).reshape(4, 128, HD)
    dk_1 = net.ring("y", lambda d: dk.at[net.coord("y", d)], lambda d: rk.at[d - 1])
    dv_1 = net.ring("y", lambda d: dv.at[net.coord("y", d)], lambda d: rv.at[d - 1])

    def d_normed_step(cols):
        part = dot(dq_out[...], wq[cols, :], NT)
        pd[:, :, :, cols] = part.astype(BF16).reshape(4, 4, 16, CHUNK)

    def gain_step(cols):
        part = pd[:, :, :, cols].reshape(TOK, CHUNK).astype(F32)
        normed = n_all[:, :, :, cols].reshape(TOK, CHUNK).astype(F32)
        gain_part[:, cols] = jnp.sum(part * normed, axis=0, keepdims=True) / gain_ref[:, cols]

    def line(axis, d, cols):
        at = net.coord(axis, d)
        return pd.at[:, at, :, cols] if axis == "y" else pd.at[at, :, :, cols]

    def reduce_far(axis, start, via):
        return [
            net.send(axis, d, line(axis, 2, pl.ds(start + n * QUART, QUART)), via.at[n])
            for n, d in enumerate((1, 3))
        ]

    def reduce_near(axis, start, near):
        out = []
        for n, d in enumerate((1, 3)):
            block = line(axis, d, pl.ds(start + (1 - n) * QUART, QUART))
            out.append(net.send(axis, d, block, near.at[n, :, :, pl.ds((1 - n) * QUART, QUART)]))
        return out

    def reduce_on(axis, start, via, relay, near, far):
        out = []
        for n, d in enumerate((1, 3)):
            far[n].wait_recv()
            at = net.coord(axis, d)

            def step(i):
                cols = pl.ds(pl.multiple_of(i * CHUNK, CHUNK), CHUNK)
                own = pl.ds(pl.multiple_of(start + n * QUART + i * CHUNK, CHUNK), CHUNK)
                mine = pd[:, at, :, own] if axis == "y" else pd[at, :, :, own]
                relay[n, :, :, cols] = (mine.astype(F32) + via[n, :, :, cols].astype(F32)).astype(BF16)

            pl.loop(0, QUART // CHUNK)(step)
            out.append(net.send(axis, d, relay.at[n], near.at[n, :, :, pl.ds(n * QUART, QUART)]))
        return out

    def reduce_end(axis, start, near, copies, into):
        arrive(copies)

        def step(i):
            cols = pl.ds(pl.multiple_of(i * CHUNK, CHUNK), CHUNK)
            own = pl.ds(pl.multiple_of(start + i * CHUNK, CHUNK), CHUNK)
            total = (pd[:, y, :, own] if axis == "y" else pd[z, :, :, own]).astype(F32)
            into[:, :, cols] = (
                total + near[0, :, :, cols].astype(F32) + near[1, :, :, cols].astype(F32)
            ).astype(BF16)

        pl.loop(0, HALF // CHUNK)(step)

    columns(0, HALF, d_normed_step)
    da_far = reduce_far("y", 0, via_a)
    columns(HALF, D, d_normed_step)
    db_far = reduce_far("z", HALF, via_b)
    arrive(dk_1)
    arrive(dv_1)
    total = dk[y].astype(F32)
    vtotal = dv[y].astype(F32)
    for d in range(3):
        total += rk[d].astype(F32)
        vtotal += rv[d].astype(F32)
    dkg[z, x, y] = total.astype(BF16)
    dvg[z, x, y] = vtotal.astype(BF16)
    mine_k, mine_v = dkg.at[z, x, y], dvg.at[z, x, y]
    dk_2 = net.send("x", 1, mine_k, mine_k)
    dv_2 = net.send("x", 1, mine_v, mine_v)
    gather_d = [
        Gather(net, lambda i, j, rows: dkg.at[i, :, j, rows], "z", "y", 0, HD),
        Gather(net, lambda i, j, rows: dvg.at[i, :, j, rows], "y", "z", 0, HD),
    ]
    dk_2.wait_recv()
    dv_2.wait_recv()
    for part in gather_d:
        part.start()
    columns(0, D, gain_step)
    for i in range(8):
        gz[z, i : i + 1, :] = gain_part[:, i * 1024 : (i + 1) * 1024]
    g_1 = net.ring("z", lambda d: gz.at[z], lambda d: gz.at[z])

    for part in gather_d:
        part.middle()
    da_near = reduce_on("y", 0, via_a, relay_a, near_a, da_far)
    for part in gather_d:
        part.spread()
    db_near = reduce_on("z", HALF, via_b, relay_b, near_b, db_far)
    for part in gather_d:
        part.forward()
    da_near += reduce_near("y", 0, near_a)
    db_near += reduce_near("z", HALF, near_b)
    feat_t[...] = feat_all[...].reshape(512, 256).astype(F32).T.astype(BF16)

    def turn_step(i):
        cols = pl.ds(pl.multiple_of(i * CHUNK, CHUNK), CHUNK)
        n_t[cols, :] = n_all[:, :, :, cols].reshape(TOK, CHUNK).astype(F32).T.astype(BF16)

    pl.loop(0, D // CHUNK)(turn_step)
    copy = pltpu.make_async_copy(n_t, n_out, local_sems.at[3])
    copy.start()
    stores.append(copy)
    arrive(g_1)
    gy[y] = (gz[0] + gz[1]) + (gz[2] + gz[3])
    g_2 = net.ring("y", lambda d: gy.at[y], lambda d: gy.at[y])

    for part in gather_d:
        part.end()
    d_feats = jnp.zeros((512, 256), F32)
    for h in range(8):
        both = jnp.concatenate(
            [full[h // 2, h % 2].reshape(512, HD) for full in (dkg, dvg)], axis=1
        )
        weights_h = jnp.concatenate(
            [wkv[:, at : at + HD] for at in (h * HD, 1024 + h * HD)], axis=1
        )
        d_feats += dot(both, weights_h, NT)
    df[...] = d_feats.astype(BF16).reshape(4, 128, 256)
    f_1 = net.ring("s", lambda d: df.at[net.coord("s", d)], lambda d: dfr.at[d - 1])
    reduce_end("y", 0, near_a, da_near, sa1)
    da_2 = net.ring("z", lambda d: sa1.at[net.coord("z", d)], lambda d: da2.at[d - 1])
    reduce_end("z", HALF, near_b, db_near, sb1)
    db_2 = net.ring("y", lambda d: sb1.at[net.coord("y", d)], lambda d: db2.at[d - 1])
    arrive(f_1)
    img = df[s].astype(F32)
    for d in range(3):
        img += dfr[d].astype(F32)
    img_s[...] = img.reshape(4, 32, 256)
    img_z[z] = img_s[z]
    f_2 = net.ring("z", lambda d: img_s.at[net.coord("z", d)], lambda d: img_z.at[z])
    for h in range(8):
        for at, full in ((h * HD, dkg), (1024 + h * HD, dvg)):
            gkv_out[:, at : at + HD] = dot(feat_t[...], full[h // 2, h % 2].reshape(512, HD)).astype(BF16)
    copy = pltpu.make_async_copy(gkv_out, gkv_hbm, local_sems.at[7])
    copy.start()
    stores.append(copy)
    arrive(g_2)
    gx2[x] = (gy[0] + gy[1]) + (gy[2] + gy[3])
    g_3 = net.send("x", 1, gx2.at[x], gx2.at[x])

    arrive(f_2)
    img_x[x] = img_z[:, pl.ds(pl.multiple_of(x * 16, 16), 16), :]
    far = pl.ds(pl.multiple_of((1 - x) * 16, 16), 16)
    f_3 = net.send("x", 1, img_z.at[:, far], img_x.at[x])
    arrive(da_2)
    arrive(db_2)

    def sum_ab(i):
        cols = pl.ds(pl.multiple_of(i * CHUNK, CHUNK), CHUNK)
        ta = sa1[z, :, cols].astype(F32)
        tb = sb1[y, :, cols].astype(F32)
        for d in range(3):
            ta += da2[d, :, cols].astype(F32)
            tb += db2[d, :, cols].astype(F32)
        own_d[:8, cols] = jnp.where(x == 0, ta[:8], ta[8:])
        own_d[8:, cols] = jnp.where(x == 0, tb[:8], tb[8:])
        fold_d[:, cols] = jnp.concatenate(
            [jnp.where(x == 0, ta[8:], ta[:8]), jnp.where(x == 0, tb[8:], tb[:8])], axis=0
        ).astype(BF16)

    pl.loop(0, HALF // CHUNK)(sum_ab)
    d_x = net.send("x", 1, fold_d, from_d)

    f_3.wait_recv()

    def tile(d):
        return pl.ds(pl.multiple_of((net.coord("y", d) // 2) * 8, 8), 8)

    gi_all[y] = img_x[:, :, tile(0), :]
    f_4 = net.ring("y", lambda d: img_x.at[:, :, tile(d)], lambda d: gi_all.at[y])
    g_3.wait_recv()
    gain = gx2[0] + gx2[1]
    for i in range(8):
        gg_out[:, i * 1024 : (i + 1) * 1024] = gain[i : i + 1]
    d_x.wait_recv()
    both = own_d[...] + from_d[...].astype(F32)
    dn = jnp.concatenate([both[:8], both[8:]], axis=1)
    xf = tok_ref[...].astype(F32)
    scaled = dn * gain_ref[...]
    gx_out[...] = (
        rinv * scaled - xf * rinv * rinv * rinv * jnp.mean(xf * scaled, axis=-1, keepdims=True)
    ).astype(BF16)
    arrive(f_4)
    for m in range(32):
        tile_m = gi_all[m % 4, (m // 4) % 2, m // 8]
        gi_out[:, m * VCOLS : (m + 1) * VCOLS] = jnp.where(y % 2 == 0, tile_m[:4], tile_m[4:])[:, :VCOLS]
    for copy in stores:
        copy.wait()
    net.finish()


def run_layer(tokens, cotangent, gain_row, visible, feats, w_q, w_o, w_kv):
    any_spec = pl.BlockSpec(memory_space=pl.ANY)
    vmem = pl.BlockSpec(memory_space=pltpu.VMEM)
    smem = pl.BlockSpec(memory_space=pltpu.SMEM)
    shape = jax.ShapeDtypeStruct
    b, f = (lambda *dims: pltpu.VMEM(dims, BF16)), (lambda *dims: pltpu.VMEM(dims, F32))
    return pl.pallas_call(
        layer_kernel,
        out_shape=(
            shape((D, 256), BF16),
            shape((4, 4, 16, D), BF16),
            shape((TOK, 256), BF16),
            shape((TOK, 256), BF16),
            shape((256, 2048), BF16),
            shape((8, D), BF16),
            shape((1, D), F32),
            shape((4, 32 * VCOLS), F32),
        ),
        in_specs=[vmem, vmem, vmem, smem, vmem, any_spec, any_spec, any_spec],
        out_specs=(any_spec,) * 5 + (vmem,) * 3,
        scratch_shapes=[
            b(256, TOK), b(TOK, 256), b(256, 2048),
            b(4, 4, 16, D), b(4, 4, 16, D), b(D, 256), b(D, 256), b(256, D), b(256, 2048),
            f(4, 2, 4, 8, HD), f(4, 4, 2, 8, HD), f(4, 4, 2, 8, HD), f(2, 4, 4, 8, HD), b(4, 128, 256),
            b(16, HALF), b(16, HALF), b(16, HALF), b(16, HALF),
            b(256, 512), f(4, 2, 4, 128, HD), b(4, 2, 4, 128, HD),
            f(2, 4, 4, 64, HD), f(2, 4, 4, 64, HD), f(2, 3, 4, 64, HD),
            f(2, 4, 64, HD), f(2, 3, 64, HD),
            b(3, 4, 2, 64, HD), b(3, 2, 4, 64, HD), f(2, 4, 2, 64, HD), f(2, 3, 2, 64, HD),
            f(2, 2, 64, HD), f(2, 64, HD),
            b(4, 128, HD), b(4, 128, HD),
            b(4, 128, HD), b(4, 128, HD), b(3, 128, HD), b(3, 128, HD),
            b(4, 2, 4, 128, HD), b(4, 2, 4, 128, HD),
            b(4, 4, 16, D),
            b(2, 4, 16, QUART), b(2, 4, 16, QUART), b(2, 4, 16, QUART), b(2, 4, 16, QUART),
            b(2, 4, 16, HALF), b(2, 4, 16, HALF),
            b(4, 16, HALF), b(4, 16, HALF),
            b(3, 16, HALF), b(3, 16, HALF),
            f(16, HALF), b(16, HALF), b(16, HALF),
            b(4, 128, 256), b(3, 128, 256),
            f(4, 32, 256), f(4, 32, 256), f(2, 4, 16, 256), f(4, 2, 4, 8, 256),
            f(1, D), f(4, 8, 1024), f(4, 8, 1024), f(2, 8, 1024),
            pltpu.SemaphoreType.DMA((NSEM,)),
            pltpu.SemaphoreType.DMA((NSEM,)),
            pltpu.SemaphoreType.DMA((8,)),
        ],
        compiler_params=pltpu.CompilerParams(
            collective_id=0, has_side_effects=True, vmem_limit_bytes=58 * 1024 * 1024
        ),
        cost_estimate=pl.CostEstimate(
            flops=6 * 10**9, bytes_accessed=20 * 2**20, transcendentals=2 * 256 * 512
        ),
        name="layer",
    )(tokens, cotangent, gain_row, visible, feats, w_q, w_o, w_kv)


def weight_kernel(nt_ref, c_ref, at_ref, dq_ref, gkv_ref, gx_ref, gg_ref, gi_ref, *outs):
    gq_out, go_out, gk_out, gx_out, gg_out, gi_out = outs
    gq_out[...] = dot(nt_ref[...], dq_ref[...]).astype(BF16)
    go_out[...] = dot(at_ref[...], c_ref[...].reshape(TOK, c_ref.shape[-1])).astype(BF16)
    gk_out[...] = gkv_ref[:VCOLS, :]
    gx_out[...] = gx_ref[...]
    gg_out[...] = gg_ref[...]
    gi_out[...] = gi_ref[...]


def weight_grads(normed_t, cotangent, attn_t, d_query, grad_kv, grad_x, grad_g, grad_image):
    steps = 2
    width, kv_width = D // steps, 2048 // steps
    shape = jax.ShapeDtypeStruct
    whole = pl.BlockSpec((TOK, 256), lambda i: (0, 0))

    def by_column(rows, cols):
        return pl.BlockSpec((rows, cols), lambda i: (0, i))

    return pl.pallas_call(
        weight_kernel,
        grid=(steps,),
        out_shape=(
            shape((D, 256), BF16),
            shape((256, D), BF16),
            shape((VCOLS, 2048), BF16),
            shape((8, D), BF16),
            shape((1, D), F32),
            shape((4, 32 * VCOLS), F32),
        ),
        in_specs=[
            pl.BlockSpec((width, 256), lambda i: (i, 0)),
            pl.BlockSpec((4, 4, 16, width), lambda i: (0, 0, 0, i)),
            whole,
            whole,
            by_column(256, kv_width),
            by_column(8, width),
            by_column(1, width),
            pl.BlockSpec((4, 32 * VCOLS), lambda i: (0, 0)),
        ],
        out_specs=(
            pl.BlockSpec((width, 256), lambda i: (i, 0)),
            by_column(256, width),
            by_column(VCOLS, kv_width),
            by_column(8, width),
            by_column(1, width),
            pl.BlockSpec((4, 32 * VCOLS), lambda i: (0, 0)),
        ),
        compiler_params=pltpu.CompilerParams(vmem_limit_bytes=62 * 1024 * 1024),
        name="weight_grads",
    )(normed_t, cotangent, attn_t, d_query, grad_kv, grad_x, grad_g, grad_image)


def per_device(tokens, upstream, norm_gain, w_query, w_output, w_keyvalue, image_feats, visible):
    results = run_layer(
        tokens[0], upstream[0], norm_gain, visible, image_feats, w_query[0], w_output[0], w_keyvalue[0]
    )
    grad_q, grad_out, grad_kv, grad_x, grad_g, grad_image = weight_grads(*results)
    return (grad_x[None], grad_g, grad_q[None], grad_out[None], grad_kv[None], grad_image)


def solution(mesh):
    placed = (
        P("section", "mp", None),
        P("section", "mp", None),
        P("section", None),
        P("section", None, "mp"),
        P("section", "mp", None),
        P("section", "mp", None),
        P(("section", "mp"), None),
        P(),
    )
    return jax.shard_map(
        per_device,
        mesh=mesh,
        in_specs=placed,
        out_specs=(
            P("section", "mp", None),
            P("section", None),
            P("section", None, "mp"),
            P("section", "mp", None),
            P("section", "mp", None),
            P(("section", "mp"), None),
        ),
        check_vma=False,
    )
```

```python
import jax
import jax.numpy as jnp
from jax import lax
from jax.experimental import pallas as pl
from jax.experimental.pallas import tpu as pltpu
from jax.sharding import PartitionSpec as P

MESH = pl.DeviceIdType.MESH
F32 = jnp.float32
BF16 = jnp.bfloat16
TOK = 256
D = 8192
HALF = D // 2
QUART = D // 4
CHUNK = 1024
HD = 128
VCOLS = 240
SCALE = HD ** (-0.5)
NSEM = 224

NT = (((1,), (1,)), ((), ()))
TN = (((0,), (0,)), ((), ()))


def dot(a, b, dims=(((1,), (0,)), ((), ()))):
    return lax.dot_general(a, b, dims, preferred_element_type=F32)


class Links:
    def __init__(self, send_sems, recv_sems):
        self.s = lax.axis_index("section")
        index = lax.axis_index("mp")
        self.z, self.x, self.y = index // 8, (index // 4) % 2, index % 4
        self.send_sems, self.recv_sems = send_sems, recv_sems
        self.copies = []

    def coord(self, axis, d):
        if axis == "x":
            return (self.x + d) % 2
        return (getattr(self, axis) + d) % 4

    def peer(self, axis, d):
        at = {"s": self.s, "z": self.z, "x": self.x, "y": self.y}
        at[axis] = self.coord(axis, d)
        return (at["s"], at["z"] * 8 + at["x"] * 4 + at["y"])

    def barrier(self):
        sem = pltpu.get_barrier_semaphore()
        peers = [(a, d) for a in ("z", "y", "s") for d in (1, 2, 3)] + [("x", 1)]
        for a, d in peers:
            pl.semaphore_signal(sem, inc=1, device_id=self.peer(a, d), device_id_type=MESH)
        return lambda: pl.semaphore_wait(sem, len(peers))

    def send(self, axis, d, src, dst):
        at = len(self.copies)
        copy = pltpu.make_async_remote_copy(
            src_ref=src,
            dst_ref=dst,
            send_sem=self.send_sems.at[at],
            recv_sem=self.recv_sems.at[at],
            device_id=self.peer(axis, d),
            device_id_type=MESH,
        )
        copy.start()
        self.copies.append(copy)
        return copy

    def ring(self, axis, src, dst):
        return [self.send(axis, d, src(d), dst(d)) for d in (1, 3, 2)]

    def finish(self):
        assert len(self.copies) <= NSEM
        for copy in self.copies:
            copy.wait_send()


def arrive(copies):
    for copy in copies:
        copy.wait_recv()


class Gather:
    def __init__(self, net, at, first, second, start, size):
        self.net, self.at, self.first, self.second = net, at, first, second
        self.cols = pl.ds(start, size)
        self.sub = (pl.ds(start, size // 2), pl.ds(start + size // 2, size // 2))

    def block(self, i, j, cols):
        i, j = self.net.coord(self.first, i), self.net.coord(self.second, j)
        return self.at(i, j, cols) if self.first == "z" else self.at(j, i, cols)

    def push(self, axis, d, i, j, cols):
        block = self.block(i, j, cols)
        return self.net.send(axis, d, block, block)

    def start(self):
        self.near = [self.push(self.first, d, 0, 0, self.cols) for d in (1, 3)]
        self.lines = [[self.push(self.second, d, 0, 0, self.cols) for d in (1, 3)]]

    def middle(self):
        self.far = []
        for copy, d, sub in zip(self.near, (1, 3), self.sub):
            copy.wait_recv()
            self.far.append(self.push(self.first, d, 4 - d, 0, sub))
            self.lines.append([self.push(self.second, e, 4 - d, 0, self.cols) for e in (1, 3)])

    def spread(self):
        arrive(self.far)
        self.lines.append([self.push(self.second, e, 2, 0, self.cols) for e in (1, 3)])

    def forward(self):
        self.last = []
        for i, line in zip((0, 3, 1, 2), self.lines):
            for copy, d, sub in zip(line, (1, 3), self.sub):
                copy.wait_recv()
                self.last.append(self.push(self.second, d, i, 4 - d, sub))

    def end(self):
        arrive(self.last)


def columns(start, stop, body, step=CHUNK):
    @pl.loop(0, (stop - start) // step)
    def _(i):
        body(pl.ds(pl.multiple_of(start + i * step, step), step))


def layer_kernel(
    tok_ref, cot_ref, gain_ref, vis_ref, feat_ref, wq_hbm, wo_hbm, wkv_hbm,
    n_out, c_out, attn_hbm, dq_hbm, gkv_hbm, gx_out, gg_out, gi_out,
    attn_out, dq_out, gkv_out,
    n_all, c_all, n_t, wq, wo, wkv,
    unit_ref, u_y, u_z, u_x, feat_all,
    fold_n, fold_c, from_n, from_c,
    feat_t, pk, pv, kx, ks0, ks1, ks2, ks3, v_y, v_z, vs1, vs2, vs3, vx, keys, values,
    dk, dv, rk, rv, dkg, dvg,
    pd, via_a, via_b, relay_a, relay_b, near_a, near_b, sa1, sb1, da2, db2, own_d, fold_d, from_d,
    df, dfr, img_s, img_z, img_x, gi_all, gain_part, gz, gy, gx2,
    send_sems, recv_sems, local_sems,
):
    net = Links(send_sems, recv_sems)
    s, z, x, y = net.s, net.z, net.x, net.y
    ready = net.barrier()
    loads = []
    wkv[VCOLS:, :] = jnp.zeros((256 - VCOLS, 2048), BF16)
    for i, (src, dst) in enumerate(((wkv_hbm, wkv.at[:VCOLS]), (wq_hbm, wq), (wo_hbm, wo))):
        copy = pltpu.make_async_copy(src, dst, local_sems.at[i])
        copy.start()
        loads.append(copy)
    xf = tok_ref[...].astype(F32)
    rinv = lax.rsqrt(jnp.mean(xf * xf, axis=-1, keepdims=True) + 1e-05)

    def normed_at(cols):
        return tok_ref[:, cols].astype(F32) * rinv * gain_ref[:, cols]

    def fold_step(at, into):
        def step(i):
            lo = pl.ds(pl.multiple_of(i * CHUNK, CHUNK), CHUNK)
            hi = pl.ds(pl.multiple_of(HALF + i * CHUNK, CHUNK), CHUNK)
            into[:, lo] = jnp.concatenate([at(lo), at(hi)], axis=0).astype(BF16)

        pl.loop(0, HALF // CHUNK)(step)

    fold_step(normed_at, fold_n)

    wide = feat_ref[...].astype(F32)
    for m in range(32):
        cols = wide[:, m * VCOLS : (m + 1) * VCOLS]
        rest = jnp.concatenate([cols[:, HD:], jnp.zeros((4, 256 - VCOLS), F32)], axis=1)
        unit_ref[m // 8, (m // 4) % 2, m % 4] = jnp.concatenate([cols[:, :HD], rest], axis=0)
    ready()
    x_n = net.send("x", 1, fold_n, from_n)
    u_y[y] = unit_ref[:, :, y]
    u_1 = net.ring("y", lambda d: unit_ref.at[:, :, net.coord("y", d)], lambda d: u_y.at[y])
    fold_step(lambda cols: cot_ref[:, cols].astype(F32), fold_c)
    x_c = net.send("x", 1, fold_c, from_c)
    arrive(u_1)
    u_z[z] = u_y[:, z]
    u_2 = net.ring("z", lambda d: u_y.at[:, net.coord("z", d)], lambda d: u_z.at[z])

    def unfold(folded, received, full):
        def step(i):
            lo = pl.ds(pl.multiple_of(i * CHUNK, CHUNK), CHUNK)
            hi = pl.ds(pl.multiple_of(HALF + i * CHUNK, CHUNK), CHUNK)
            mine = folded[:, lo].astype(F32)
            other = received[:, lo].astype(F32)
            for at, cols in ((0, lo), (8, hi)):
                a, b = mine[at : at + 8], other[at : at + 8]
                first = jnp.where(x == 0, a, b)
                second = jnp.where(x == 0, b, a)
                full[z, y, :, cols] = jnp.concatenate([first, second], axis=0).astype(BF16)

        pl.loop(0, HALF // CHUNK)(step)

    a_cols, b_cols = pl.ds(0, HALF), pl.ds(HALF, HALF)
    def gathers(full):
        at = lambda i, j, cols: full.at[i, j, :, cols]
        return [Gather(net, at, "z", "y", 0, HALF), Gather(net, at, "y", "z", HALF, HALF)]

    gather_n, gather_c = gathers(n_all), gathers(c_all)
    x_n.wait_recv()
    unfold(fold_n, from_n, n_all)
    for half in gather_n:
        half.start()

    arrive(u_2)
    u_x[x] = u_z[:, :, x]
    u_3 = net.send("x", 1, u_z.at[:, :, 1 - x], u_x.at[x])
    x_c.wait_recv()
    unfold(fold_c, from_c, c_all)
    for half in gather_n:
        half.middle()

    u_3.wait_recv()
    units = u_x[...].reshape(256, HD).astype(BF16)
    row = lax.broadcasted_iota(jnp.int32, (128, 256), 0)
    col = lax.broadcasted_iota(jnp.int32, (128, 256), 1)
    at = (((row // 16) % 2 * 4 + row // 32) * 4 + (row // 4) % 4) * 8 + row % 4
    for half in range(2):
        pick = jnp.where(col == at + 4 * half, 1.0, 0.0).astype(BF16)
        feat_all[s, :, half * HD : (half + 1) * HD] = dot(pick, units).astype(BF16)
    f_0 = net.ring("s", lambda d: feat_all.at[s], lambda d: feat_all.at[s])
    for half in gather_n:
        half.spread()
    arrive(f_0)

    loads[0].wait()

    def kv_step(h):
        cols = pl.ds(pl.multiple_of(h * HD, HD), HD)
        vcols = pl.ds(pl.multiple_of(1024 + h * HD, HD), HD)
        feats = feat_all[...].reshape(512, 256)
        pk[h // 2, h % 2] = dot(feats, wkv[:, cols]).reshape(4, 128, HD)
        pv[h // 2, h % 2] = dot(feats, wkv[:, vcols]).astype(BF16).reshape(4, 128, HD)

    pl.loop(0, 8)(kv_step)

    axes = (("y", "z"), ("z", "y"))
    halves = [pl.ds(0, 64), pl.ds(64, 64)]

    def along(n, level, ref, d):
        axis = axes[n][level]
        at = net.coord(axis, d)
        return ref.at[:, at] if level == 0 and n == 0 else ref.at[at]

    k_x = [net.send("x", 1, pk.at[:, 1 - x, :, rows], kx.at[n]) for n, rows in enumerate(halves)]
    v_1 = [
        net.ring("y", lambda d: pv.at[:, :, net.coord("y", d), halves[0]], lambda d: v_y.at[d - 1]),
        net.ring("z", lambda d: pv.at[net.coord("z", d), :, :, halves[1]], lambda d: v_z.at[d - 1]),
    ]
    for half in gather_n:
        half.forward()
    for half in gather_c:
        half.start()

    v_2 = []
    for n in range(2):
        arrive(v_1[n])
        for a in range(4):
            for b in range(2):
                total = (pv[a, b, y, halves[0]] if n == 0 else pv[z, b, a, halves[1]]).astype(F32)
                for d in range(3):
                    total += (v_y[d, a, b] if n == 0 else v_z[d, b, a]).astype(F32)
                vs1[n, a, b] = total
        v_2.append(
            net.ring(axes[n][1], lambda d: along(n, 1, vs1.at[n], d), lambda d: vs2.at[n, d - 1])
        )
    for half in gather_c:
        half.middle()
    for half in gather_n:
        half.end()
    loads[1].wait()

    def query_step(i, acc):
        cols = pl.ds(pl.multiple_of(i * CHUNK, CHUNK), CHUNK)
        return acc + dot(n_all[:, :, :, cols].reshape(TOK, CHUNK), wq[cols, :])

    query = lax.fori_loop(0, D // CHUNK, query_step, jnp.zeros((TOK, 256), F32)).astype(BF16)
    for half in gather_c:
        half.spread()
    k_2 = []
    for n, rows in enumerate(halves):
        k_x[n].wait_recv()
        for a in range(4):
            ks0[n, a] = pk[a, x, :, rows] + kx[n, a]
        k_2.append(
            net.ring(axes[n][0], lambda d: along(n, 0, ks0.at[n], d), lambda d: ks1.at[n, d - 1])
        )
    v_x = []
    for n in range(2):
        arrive(v_2[n])
        mine = net.coord(axes[n][1], 0)
        for b in range(2):
            total = vs1[n, mine, b]
            for d in range(3):
                total += vs2[n, d, b]
            vs3[n, b] = total
        v_x.append(net.send("x", 1, vs3.at[n, 1 - x], vx.at[n]))
    k_3 = []
    for n in range(2):
        arrive(k_2[n])
        for a in range(4):
            total = ks0[n, a, y] if n == 0 else ks0[n, z, a]
            for d in range(3):
                total += ks1[n, d, a]
            ks2[n, a] = total
        k_3.append(
            net.ring(axes[n][1], lambda d: along(n, 1, ks2.at[n], d), lambda d: ks3.at[n, d - 1])
        )
    for half in gather_c:
        half.forward()
    for n in range(2):
        v_x[n].wait_recv()
        values[y, 64 * n : 64 * n + 64] = (vs3[n, x] + vx[n]).astype(BF16)
    v_3 = net.ring("y", lambda d: values.at[y], lambda d: values.at[y])
    for n in range(2):
        arrive(k_3[n])
        total = ks2[n, net.coord(axes[n][1], 0)]
        for d in range(3):
            total += ks3[n, d]
        keys[y, 64 * n : 64 * n + 64] = total.astype(BF16)
    k_3 = net.ring("y", lambda d: keys.at[y], lambda d: keys.at[y])

    stores = []
    arrive(k_3)
    arrive(v_3)
    key = keys[...].reshape(512, HD)
    value = values[...].reshape(512, HD)
    image_of = lax.broadcasted_iota(jnp.int32, (TOK, 512), 1) // 128
    late = lax.broadcasted_iota(jnp.int32, (TOK, 512), 0) >= 128
    allowed = image_of < jnp.where(late, vis_ref[1], vis_ref[0])
    probs, weights = [], []
    for j in range(2):
        q = query[:, j * HD : (j + 1) * HD]
        scores = jnp.where(allowed, dot(q, key, NT) * SCALE, -1e30)
        expo = jnp.exp(scores - jnp.max(scores, axis=-1, keepdims=True))
        prob = expo / jnp.sum(expo, axis=-1, keepdims=True)
        probs.append(prob)
        weights.append(prob.astype(BF16))
        attn = dot(weights[j], value).astype(BF16)
        attn_out[j * HD : (j + 1) * HD, :] = attn.astype(F32).T.astype(BF16)

    for half in gather_c:
        half.end()
    copy = pltpu.make_async_copy(c_all, c_out, local_sems.at[4])
    copy.start()
    stores.append(copy)
    loads[2].wait()

    def d_attn_step(i, acc):
        cols = pl.ds(pl.multiple_of(i * CHUNK, CHUNK), CHUNK)
        return acc + dot(c_all[:, :, :, cols].reshape(TOK, CHUNK), wo[:, cols], NT)

    d_attn = lax.fori_loop(0, D // CHUNK, d_attn_step, jnp.zeros((TOK, 256), F32)).astype(BF16)
    d_key = jnp.zeros((512, HD), F32)
    d_value = jnp.zeros((512, HD), F32)
    for j in range(2):
        heads = slice(j * HD, (j + 1) * HD)
        da = d_attn[:, heads]
        d_prob = dot(da, value, NT)
        delta = jnp.sum(probs[j] * d_prob, axis=-1, keepdims=True)
        d_score = (probs[j] * (d_prob - delta) * SCALE).astype(BF16)
        dq_out[:, heads] = dot(d_score, key).astype(BF16)
        d_key += dot(d_score, query[:, heads], TN)
        d_value += dot(weights[j], da, TN)
    for i, (src, dst) in enumerate(((attn_out, attn_hbm), (dq_out, dq_hbm))):
        copy = pltpu.make_async_copy(src, dst, local_sems.at[5 + i])
        copy.start()
        stores.append(copy)
    dk[...] = d_key.astype(BF16).reshape(4, 128, HD)
    dv[...] = d_value.astype(BF16).reshape(4, 128, HD)
    dk_1 = net.ring("y", lambda d: dk.at[net.coord("y", d)], lambda d: rk.at[d - 1])
    dv_1 = net.ring("y", lambda d: dv.at[net.coord("y", d)], lambda d: rv.at[d - 1])

    def d_normed_step(cols):
        part = dot(dq_out[...], wq[cols, :], NT)
        pd[:, :, :, cols] = part.astype(BF16).reshape(4, 4, 16, CHUNK)

    def gain_step(cols):
        part = pd[:, :, :, cols].reshape(TOK, CHUNK).astype(F32)
        normed = n_all[:, :, :, cols].reshape(TOK, CHUNK).astype(F32)
        gain_part[:, cols] = jnp.sum(part * normed, axis=0, keepdims=True) / gain_ref[:, cols]

    def line(axis, d, cols):
        at = net.coord(axis, d)
        return pd.at[:, at, :, cols] if axis == "y" else pd.at[at, :, :, cols]

    def reduce_far(axis, start, via):
        return [
            net.send(axis, d, line(axis, 2, pl.ds(start + n * QUART, QUART)), via.at[n])
            for n, d in enumerate((1, 3))
        ]

    def reduce_near(axis, start, near):
        out = []
        for n, d in enumerate((1, 3)):
            block = line(axis, d, pl.ds(start + (1 - n) * QUART, QUART))
            out.append(net.send(axis, d, block, near.at[n, :, :, pl.ds((1 - n) * QUART, QUART)]))
        return out

    def reduce_on(axis, start, via, relay, near, far):
        out = []
        for n, d in enumerate((1, 3)):
            far[n].wait_recv()
            at = net.coord(axis, d)

            def step(i):
                cols = pl.ds(pl.multiple_of(i * CHUNK, CHUNK), CHUNK)
                own = pl.ds(pl.multiple_of(start + n * QUART + i * CHUNK, CHUNK), CHUNK)
                mine = pd[:, at, :, own] if axis == "y" else pd[at, :, :, own]
                relay[n, :, :, cols] = (mine.astype(F32) + via[n, :, :, cols].astype(F32)).astype(BF16)

            pl.loop(0, QUART // CHUNK)(step)
            out.append(net.send(axis, d, relay.at[n], near.at[n, :, :, pl.ds(n * QUART, QUART)]))
        return out

    def reduce_end(axis, start, near, copies, into):
        arrive(copies)

        def step(i):
            cols = pl.ds(pl.multiple_of(i * CHUNK, CHUNK), CHUNK)
            own = pl.ds(pl.multiple_of(start + i * CHUNK, CHUNK), CHUNK)
            total = (pd[:, y, :, own] if axis == "y" else pd[z, :, :, own]).astype(F32)
            into[:, :, cols] = (
                total + near[0, :, :, cols].astype(F32) + near[1, :, :, cols].astype(F32)
            ).astype(BF16)

        pl.loop(0, HALF // CHUNK)(step)

    columns(0, HALF, d_normed_step)
    da_far = reduce_far("y", 0, via_a)
    columns(HALF, D, d_normed_step)
    db_far = reduce_far("z", HALF, via_b)
    columns(0, D, gain_step)
    for i in range(8):
        gz[z, i : i + 1, :] = gain_part[:, i * 1024 : (i + 1) * 1024]
    g_1 = net.ring("z", lambda d: gz.at[z], lambda d: gz.at[z])
    arrive(dk_1)
    arrive(dv_1)
    total = dk[y].astype(F32)
    vtotal = dv[y].astype(F32)
    for d in range(3):
        total += rk[d].astype(F32)
        vtotal += rv[d].astype(F32)
    dkg[z, x, y] = total.astype(BF16)
    dvg[z, x, y] = vtotal.astype(BF16)
    mine_k, mine_v = dkg.at[z, x, y], dvg.at[z, x, y]
    dk_2 = net.send("x", 1, mine_k, mine_k)
    dv_2 = net.send("x", 1, mine_v, mine_v)
    gather_d = [
        Gather(net, lambda i, j, rows: dkg.at[i, :, j, rows], "z", "y", 0, HD),
        Gather(net, lambda i, j, rows: dvg.at[i, :, j, rows], "y", "z", 0, HD),
    ]
    dk_2.wait_recv()
    dv_2.wait_recv()
    for part in gather_d:
        part.start()
    for part in gather_d:
        part.middle()
    da_near = reduce_on("y", 0, via_a, relay_a, near_a, da_far)
    for part in gather_d:
        part.spread()
    db_near = reduce_on("z", HALF, via_b, relay_b, near_b, db_far)
    for part in gather_d:
        part.forward()
    da_near += reduce_near("y", 0, near_a)
    db_near += reduce_near("z", HALF, near_b)
    feat_t[...] = feat_all[...].reshape(512, 256).astype(F32).T.astype(BF16)

    def turn_step(i):
        cols = pl.ds(pl.multiple_of(i * CHUNK, CHUNK), CHUNK)
        n_t[cols, :] = n_all[:, :, :, cols].reshape(TOK, CHUNK).astype(F32).T.astype(BF16)

    pl.loop(0, D // CHUNK)(turn_step)
    copy = pltpu.make_async_copy(n_t, n_out, local_sems.at[3])
    copy.start()
    stores.append(copy)
    arrive(g_1)
    gy[y] = (gz[0] + gz[1]) + (gz[2] + gz[3])
    g_2 = net.ring("y", lambda d: gy.at[y], lambda d: gy.at[y])

    for part in gather_d:
        part.end()
    d_feats = jnp.zeros((512, 256), F32)
    for h in range(8):
        both = jnp.concatenate(
            [full[h // 2, h % 2].reshape(512, HD) for full in (dkg, dvg)], axis=1
        )
        weights_h = jnp.concatenate(
            [wkv[:, at : at + HD] for at in (h * HD, 1024 + h * HD)], axis=1
        )
        d_feats += dot(both, weights_h, NT)
    df[...] = d_feats.astype(BF16).reshape(4, 128, 256)
    f_1 = net.ring("s", lambda d: df.at[net.coord("s", d)], lambda d: dfr.at[d - 1])
    reduce_end("y", 0, near_a, da_near, sa1)
    da_2 = net.ring("z", lambda d: sa1.at[net.coord("z", d)], lambda d: da2.at[d - 1])
    reduce_end("z", HALF, near_b, db_near, sb1)
    db_2 = net.ring("y", lambda d: sb1.at[net.coord("y", d)], lambda d: db2.at[d - 1])
    arrive(f_1)
    img = df[s].astype(F32)
    for d in range(3):
        img += dfr[d].astype(F32)
    img_s[...] = img.reshape(4, 32, 256)
    img_z[z] = img_s[z]
    f_2 = net.ring("z", lambda d: img_s.at[net.coord("z", d)], lambda d: img_z.at[z])
    for h in range(8):
        for at, full in ((h * HD, dkg), (1024 + h * HD, dvg)):
            gkv_out[:, at : at + HD] = dot(feat_t[...], full[h // 2, h % 2].reshape(512, HD)).astype(BF16)
    copy = pltpu.make_async_copy(gkv_out, gkv_hbm, local_sems.at[7])
    copy.start()
    stores.append(copy)
    arrive(g_2)
    gx2[x] = (gy[0] + gy[1]) + (gy[2] + gy[3])
    g_3 = net.send("x", 1, gx2.at[x], gx2.at[x])

    arrive(f_2)
    img_x[x] = img_z[:, pl.ds(pl.multiple_of(x * 16, 16), 16), :]
    far = pl.ds(pl.multiple_of((1 - x) * 16, 16), 16)
    f_3 = net.send("x", 1, img_z.at[:, far], img_x.at[x])
    arrive(da_2)
    arrive(db_2)

    def sum_ab(i):
        cols = pl.ds(pl.multiple_of(i * CHUNK, CHUNK), CHUNK)
        ta = sa1[z, :, cols].astype(F32)
        tb = sb1[y, :, cols].astype(F32)
        for d in range(3):
            ta += da2[d, :, cols].astype(F32)
            tb += db2[d, :, cols].astype(F32)
        own_d[:8, cols] = jnp.where(x == 0, ta[:8], ta[8:])
        own_d[8:, cols] = jnp.where(x == 0, tb[:8], tb[8:])
        fold_d[:, cols] = jnp.concatenate(
            [jnp.where(x == 0, ta[8:], ta[:8]), jnp.where(x == 0, tb[8:], tb[:8])], axis=0
        ).astype(BF16)

    pl.loop(0, HALF // CHUNK)(sum_ab)
    d_x = net.send("x", 1, fold_d, from_d)

    f_3.wait_recv()

    def tile(d):
        return pl.ds(pl.multiple_of((net.coord("y", d) // 2) * 8, 8), 8)

    gi_all[y] = img_x[:, :, tile(0), :]
    f_4 = net.ring("y", lambda d: img_x.at[:, :, tile(d)], lambda d: gi_all.at[y])
    g_3.wait_recv()
    gain = gx2[0] + gx2[1]
    for i in range(8):
        gg_out[:, i * 1024 : (i + 1) * 1024] = gain[i : i + 1]
    d_x.wait_recv()
    both = own_d[...] + from_d[...].astype(F32)
    dn = jnp.concatenate([both[:8], both[8:]], axis=1)
    xf = tok_ref[...].astype(F32)
    scaled = dn * gain_ref[...]
    gx_out[...] = (
        rinv * scaled - xf * rinv * rinv * rinv * jnp.mean(xf * scaled, axis=-1, keepdims=True)
    ).astype(BF16)
    arrive(f_4)
    for m in range(32):
        tile_m = gi_all[m % 4, (m // 4) % 2, m // 8]
        gi_out[:, m * VCOLS : (m + 1) * VCOLS] = jnp.where(y % 2 == 0, tile_m[:4], tile_m[4:])[:, :VCOLS]
    for copy in stores:
        copy.wait()
    net.finish()


def run_layer(tokens, cotangent, gain_row, visible, feats, w_q, w_o, w_kv):
    any_spec = pl.BlockSpec(memory_space=pl.ANY)
    vmem = pl.BlockSpec(memory_space=pltpu.VMEM)
    smem = pl.BlockSpec(memory_space=pltpu.SMEM)
    shape = jax.ShapeDtypeStruct
    b, f = (lambda *dims: pltpu.VMEM(dims, BF16)), (lambda *dims: pltpu.VMEM(dims, F32))
    return pl.pallas_call(
        layer_kernel,
        out_shape=(
            shape((D, 256), BF16),
            shape((4, 4, 16, D), BF16),
            shape((TOK, 256), BF16),
            shape((TOK, 256), BF16),
            shape((256, 2048), BF16),
            shape((8, D), BF16),
            shape((1, D), F32),
            shape((4, 32 * VCOLS), F32),
        ),
        in_specs=[vmem, vmem, vmem, smem, vmem, any_spec, any_spec, any_spec],
        out_specs=(any_spec,) * 5 + (vmem,) * 3,
        scratch_shapes=[
            b(256, TOK), b(TOK, 256), b(256, 2048),
            b(4, 4, 16, D), b(4, 4, 16, D), b(D, 256), b(D, 256), b(256, D), b(256, 2048),
            f(4, 2, 4, 8, HD), f(4, 4, 2, 8, HD), f(4, 4, 2, 8, HD), f(2, 4, 4, 8, HD), b(4, 128, 256),
            b(16, HALF), b(16, HALF), b(16, HALF), b(16, HALF),
            b(256, 512), f(4, 2, 4, 128, HD), b(4, 2, 4, 128, HD),
            f(2, 4, 4, 64, HD), f(2, 4, 4, 64, HD), f(2, 3, 4, 64, HD),
            f(2, 4, 64, HD), f(2, 3, 64, HD),
            b(3, 4, 2, 64, HD), b(3, 2, 4, 64, HD), f(2, 4, 2, 64, HD), f(2, 3, 2, 64, HD),
            f(2, 2, 64, HD), f(2, 64, HD),
            b(4, 128, HD), b(4, 128, HD),
            b(4, 128, HD), b(4, 128, HD), b(3, 128, HD), b(3, 128, HD),
            b(4, 2, 4, 128, HD), b(4, 2, 4, 128, HD),
            b(4, 4, 16, D),
            b(2, 4, 16, QUART), b(2, 4, 16, QUART), b(2, 4, 16, QUART), b(2, 4, 16, QUART),
            b(2, 4, 16, HALF), b(2, 4, 16, HALF),
            b(4, 16, HALF), b(4, 16, HALF),
            b(3, 16, HALF), b(3, 16, HALF),
            f(16, HALF), b(16, HALF), b(16, HALF),
            b(4, 128, 256), b(3, 128, 256),
            f(4, 32, 256), f(4, 32, 256), f(2, 4, 16, 256), f(4, 2, 4, 8, 256),
            f(1, D), f(4, 8, 1024), f(4, 8, 1024), f(2, 8, 1024),
            pltpu.SemaphoreType.DMA((NSEM,)),
            pltpu.SemaphoreType.DMA((NSEM,)),
            pltpu.SemaphoreType.DMA((8,)),
        ],
        compiler_params=pltpu.CompilerParams(
            collective_id=0, has_side_effects=True, vmem_limit_bytes=58 * 1024 * 1024
        ),
        cost_estimate=pl.CostEstimate(
            flops=6 * 10**9, bytes_accessed=20 * 2**20, transcendentals=2 * 256 * 512
        ),
        name="layer",
    )(tokens, cotangent, gain_row, visible, feats, w_q, w_o, w_kv)


def weight_kernel(nt_ref, c_ref, at_ref, dq_ref, gkv_ref, gx_ref, gg_ref, gi_ref, *outs):
    gq_out, go_out, gk_out, gx_out, gg_out, gi_out = outs
    gq_out[...] = dot(nt_ref[...], dq_ref[...]).astype(BF16)
    go_out[...] = dot(at_ref[...], c_ref[...].reshape(TOK, c_ref.shape[-1])).astype(BF16)
    gk_out[...] = gkv_ref[:VCOLS, :]
    gx_out[...] = gx_ref[...]
    gg_out[...] = gg_ref[...]
    gi_out[...] = gi_ref[...]


def weight_grads(normed_t, cotangent, attn_t, d_query, grad_kv, grad_x, grad_g, grad_image):
    steps = 2
    width, kv_width = D // steps, 2048 // steps
    shape = jax.ShapeDtypeStruct
    whole = pl.BlockSpec((TOK, 256), lambda i: (0, 0))

    def by_column(rows, cols):
        return pl.BlockSpec((rows, cols), lambda i: (0, i))

    return pl.pallas_call(
        weight_kernel,
        grid=(steps,),
        out_shape=(
            shape((D, 256), BF16),
            shape((256, D), BF16),
            shape((VCOLS, 2048), BF16),
            shape((8, D), BF16),
            shape((1, D), F32),
            shape((4, 32 * VCOLS), F32),
        ),
        in_specs=[
            pl.BlockSpec((width, 256), lambda i: (i, 0)),
            pl.BlockSpec((4, 4, 16, width), lambda i: (0, 0, 0, i)),
            whole,
            whole,
            by_column(256, kv_width),
            by_column(8, width),
            by_column(1, width),
            pl.BlockSpec((4, 32 * VCOLS), lambda i: (0, 0)),
        ],
        out_specs=(
            pl.BlockSpec((width, 256), lambda i: (i, 0)),
            by_column(256, width),
            by_column(VCOLS, kv_width),
            by_column(8, width),
            by_column(1, width),
            pl.BlockSpec((4, 32 * VCOLS), lambda i: (0, 0)),
        ),
        compiler_params=pltpu.CompilerParams(vmem_limit_bytes=62 * 1024 * 1024),
        name="weight_grads",
    )(normed_t, cotangent, attn_t, d_query, grad_kv, grad_x, grad_g, grad_image)


def per_device(tokens, upstream, norm_gain, w_query, w_output, w_keyvalue, image_feats, visible):
    results = run_layer(
        tokens[0], upstream[0], norm_gain, visible, image_feats, w_query[0], w_output[0], w_keyvalue[0]
    )
    grad_q, grad_out, grad_kv, grad_x, grad_g, grad_image = weight_grads(*results)
    return (grad_x[None], grad_g, grad_q[None], grad_out[None], grad_kv[None], grad_image)


def solution(mesh):
    placed = (
        P("section", "mp", None),
        P("section", "mp", None),
        P("section", None),
        P("section", None, "mp"),
        P("section", "mp", None),
        P("section", "mp", None),
        P(("section", "mp"), None),
        P(),
    )
    return jax.shard_map(
        per_device,
        mesh=mesh,
        in_specs=placed,
        out_specs=(
            P("section", "mp", None),
            P("section", None),
            P("section", None, "mp"),
            P("section", "mp", None),
            P("section", "mp", None),
            P(("section", "mp"), None),
        ),
        check_vma=False,
    )
```
